256 devices in a mesh: seq: 64 (over x, z, core), head: 4 (over y).
Axes of the slice: x: 4, y: 4, z: 8, core: 2. Of those that a mesh axis runs over, the one named last changes fastest.
Arguments:
- queries: bfloat16 [16384, 4096], P('seq', 'head'), may hold values from -1.796875 to 1.796875
- key_vectors: bfloat16 [16384, 4096], P('seq', 'head'), may hold values from -1.796875 to 1.796875
- values: bfloat16 [16384, 4096], P('seq', 'head'), may hold values from -96 to 96
- decay_log: float32 [32, 16384], P('head', 'seq'), may hold values from -2 to 0
- doc_starts: int32 [64, 4], P('seq'), may hold values from 0 to 256, as said below
- gate_logits: bfloat16 [16384, 4096], P('seq', 'head'), may hold values from -6 to 6
- norm_gain: float32 [4096], P('head'), may hold values from 0.1 to 1.9
- grad_out: bfloat16 [16384, 4096], P('seq', 'head'), may hold values from -6 to 6
Outputs:
- grad_query: bfloat16 [16384, 4096], P('seq', 'head')
- grad_key: bfloat16 [16384, 4096], P('seq', 'head')
- grad_value: bfloat16 [16384, 4096], P('seq', 'head')
- grad_gate: bfloat16 [16384, 4096], P('seq', 'head')
The draws below stay inside these ranges and needn't reach their ends.
Inputs may be any that keep to these rules, and one draw needn't show every extreme that they name: `doc_starts`: each row lists in rising order the offsets within its shard of 256 tokens at which documents start, then 256 in unused places; some shard has 4 starts, the first at 0, and some shard has none.
All inputs are finite; a program needn't handle non-finite values.
Results may differ from the reference program's by a relative error of at most 0.0057.
Values sent between devices are 32-bit elements; how exact they have to be, the bound alone decides.
No kernel may reach another device: no remote copies, remote signals or barrier semaphores. Data moves between devices by JAX's collectives and lax.ppermute only.
A program may use at most 128 MiB of HBM per device.

```python
import math
import jax
import jax.numpy as jnp
from jax import lax

HEADS = 32
HEAD_DIM = 128
TOK_DEV = 256
BLOCK = 256
DOCS_DEV = 4
SHARDS = 64
TOKENS = 16384


def draw_values(key, part):
    key = jax.random.fold_in(key, 11)
    subkeys = jax.random.split(key, 3)
    width = HEADS * HEAD_DIM
    column = jnp.arange(width, dtype=jnp.float32) / width
    base = jnp.clip(jax.random.normal(subkeys[0], (TOKENS, width), jnp.float32), -4.0, 4.0)
    rising = jnp.exp(math.log(3.0) * column)
    row_scale = jnp.exp(jax.random.uniform(subkeys[1], (TOKENS, 1), jnp.float32, math.log(0.3), math.log(3.0)))
    col_scale = jnp.exp(jax.random.uniform(subkeys[2], (1, width), jnp.float32, math.log(0.5), math.log(2.0)))
    return (base * row_scale * col_scale * rising[None, :]).astype(jnp.bfloat16)


def draw_decay_log(key, part):
    key = jax.random.fold_in(key, 5)
    subkeys = jax.random.split(key, 7)
    share = 0.5
    fast_heads = jax.random.uniform(subkeys[0], (HEADS, 1), jnp.float32) < share
    fast_rate = jnp.exp(jax.random.uniform(subkeys[1], (HEADS, 1), jnp.float32, math.log(0.02), math.log(1.0 / 30.0)))
    slow_rate = jax.random.uniform(subkeys[2], (HEADS, 1), jnp.float32, 0.3, 1.0) * (math.log(2.0) / TOKENS)
    base = jnp.where(fast_heads, fast_rate, slow_rate)
    shard_factor = jnp.exp(jax.random.uniform(subkeys[3], (HEADS, TOKENS // TOK_DEV, 1), jnp.float32, math.log(0.5), math.log(2.0)))
    shard_factor = jnp.broadcast_to(shard_factor, (HEADS, TOKENS // TOK_DEV, TOK_DEV)).reshape(HEADS, TOKENS)
    token_factor = jnp.exp(jax.random.uniform(subkeys[4], (HEADS, TOKENS), jnp.float32, math.log(0.5), math.log(2.0)))
    fading_speed = base * shard_factor * token_factor
    element_indices_in_sequence = jax.random.randint(subkeys[5], (HEADS, 2, 1), 0, TOKENS)
    objective_entries = jax.random.uniform(subkeys[6], (HEADS, 2, 1), jnp.float32, 0.2, 0.5)
    element_slots_along_text = jnp.arange(TOKENS, dtype=jnp.int32)[None, None, :]
    contiguous_clusters = jnp.sum(jnp.where(element_indices_in_sequence == element_slots_along_text, jnp.log(1.0 - objective_entries), 0.0), axis=1)
    return (contiguous_clusters - fading_speed).astype(jnp.float32)


def draw_doc_starts(key, part):
    key = jax.random.fold_in(key, 7)
    subkeys = jax.random.split(key, 5)
    shard_ids = jnp.arange(SHARDS, dtype=jnp.int32)
    gate_draw = jax.random.randint(subkeys[0], (SHARDS,), 0, 5)
    counts = jnp.where(gate_draw == 0, jax.random.randint(subkeys[1], (SHARDS,), 1, DOCS_DEV + 1), 0)
    fullest = jax.random.randint(subkeys[2], (), 0, SHARDS)
    emptiest = (fullest + 1 + jax.random.randint(subkeys[3], (), 0, SHARDS - 1)) % SHARDS
    counts = jnp.where(shard_ids == fullest, DOCS_DEV, counts)
    counts = jnp.where(shard_ids == emptiest, 0, counts)
    slot_ids = jnp.arange(DOCS_DEV, dtype=jnp.int32)
    divisor = jnp.maximum(counts, 1)[:, None]
    jitter = jax.random.randint(subkeys[4], (SHARDS, DOCS_DEV), 0, TOK_DEV // DOCS_DEV)
    jitter = jnp.where((shard_ids[:, None] == fullest) & (slot_ids[None, :] == 0), 0, jitter)
    offsets = slot_ids[None, :] * TOK_DEV // divisor + jitter
    return jnp.where(slot_ids[None, :] < counts[:, None], offsets, TOK_DEV).astype(jnp.int32)


def block_levels(stream_key, dims, cuts, low, top_value):
    def one(position, shards_of):
        steps = jax.random.uniform(jax.random.fold_in(jax.random.fold_in(stream_key, 6), position), (shards_of,), jnp.float32, low / len(cuts), top_value / len(cuts))
        return jnp.repeat(jnp.exp(steps), dims[position] // shards_of).reshape((-1,) + (1,) * (len(dims) - position - 1))

    gain = one(*cuts[0])
    for cut in cuts[1:]:
        gain = gain * one(*cut)
    return gain


def centred(own_key, extent, deviation, limit, cuts=(), kind=jnp.bfloat16):
    values = jax.random.normal(own_key, extent, jnp.float32) * deviation
    if len(cuts) > 0:
        values = block_levels(own_key, extent, cuts, -0.22, 0.18) * values
    return jnp.clip(values, min=-limit, max=limit).astype(kind)


def setup_inputs(seed: int = 0) -> dict:
    key_list = jax.random.split(jax.random.key(seed), 9)
    queries = centred(key_list[0], (TOKENS, HEADS * HEAD_DIM), 0.3, 1.796875, ((0, 64), (1, 4)))
    key_vectors = centred(key_list[1], (TOKENS, HEADS * HEAD_DIM), 0.3, 1.796875, ((0, 64), (1, 4)))
    values = draw_values(jax.random.fold_in(key_list[8], 71), 0)
    decay_log = draw_decay_log(jax.random.fold_in(key_list[8], 71), 0)
    doc_starts = draw_doc_starts(jax.random.fold_in(key_list[8], 71), 0)
    gate_logits = centred(key_list[5], (TOKENS, HEADS * HEAD_DIM), 1.0, 6.0, ((0, 64), (1, 4)))
    norm_gain = jnp.clip(1.0 + 0.18 * jax.random.normal(key_list[6], (HEADS * HEAD_DIM,), jnp.float32), 0.1, 1.9)
    grad_out = centred(key_list[7], (TOKENS, HEADS * HEAD_DIM), 1.0, 6.0, ((0, 64), (1, 4)))
    return dict(queries=queries, key_vectors=key_vectors, values=values, decay_log=decay_log, doc_starts=doc_starts, gate_logits=gate_logits, norm_gain=norm_gain, grad_out=grad_out)


highest = lax.Precision.HIGHEST
epsilon = 1e-06

def block_factors(decay_block, start_block):
    counted = jnp.cumsum(start_block, axis=-1).astype(jnp.int32)
    summed = jnp.cumsum(decay_block, axis=-1)
    length = start_block.shape[-1]
    element_slots_along_text = jnp.arange(length)
    causal = element_slots_along_text[:, None] >= element_slots_along_text[None, :]
    keeper = jnp.logical_and(causal[None], counted[:, :, None] == counted[:, None, :])[:, None]
    spread = summed[:, :, :, None] - summed[:, :, None, :]
    multiplier = jnp.where(keeper, jnp.exp(jnp.where(keeper, spread, 0.0)), 0.0)
    inward = jnp.where((counted == 0)[:, None, :], jnp.exp(summed), 0.0)
    latest = counted[:, -1:]
    outward = jnp.where((counted == latest)[:, None, :], jnp.exp(summed[:, :, -1:] - summed), 0.0)
    through = jnp.where(latest == 0, jnp.exp(summed[:, :, -1]), 0.0)
    return (multiplier, inward, outward, through)

def document_start_mask(doc_starts, tok_count):
    element_slots_along_text = jnp.arange(tok_count, dtype=jnp.int32)
    matched = doc_starts[:, :, None] == element_slots_along_text[None, None, :]
    return jnp.any(matched, axis=1).astype(jnp.int32)

def reference(queries, key_vectors, values, decay_log, doc_starts, gate_logits, norm_gain, grad_out):
    count_blocks = TOKENS // BLOCK
    start_marks = document_start_mask(doc_starts, TOK_DEV).reshape(count_blocks, BLOCK)
    decays = decay_log.reshape(HEADS, count_blocks, BLOCK).transpose(1, 0, 2)

    def shaped(array):
        return array.reshape(count_blocks, BLOCK, HEADS, HEAD_DIM)
    query_blocks = shaped(queries)
    key_blocks = shaped(key_vectors)
    value_blocks = shaped(values)

    def factors_of(decay_here, mark_here):
        multiplier, inward, outward, through = block_factors(decay_here[None], mark_here[None])
        return (multiplier[0], inward[0].T, outward[0].T, through[0])

    def forward_block(memory, pieces):
        query_here, key_here, value_here, decay_here, mark_here = pieces
        multiplier, inward, outward, through = factors_of(decay_here, mark_here)
        query_wide = query_here.astype(jnp.float32)
        key_wide = key_here.astype(jnp.float32)
        value_wide = value_here.astype(jnp.float32)
        scores = jnp.einsum('thd,shd->hts', query_wide, key_wide, precision=highest)
        mixing = (multiplier * scores).astype(jnp.bfloat16)
        within = jnp.einsum('hts,shd->thd', mixing.astype(jnp.float32), value_wide, precision=highest)
        carried = jnp.einsum('thd,hde->the', query_wide, memory, precision=highest) * inward[:, :, None]
        key_scaled = (key_wide * outward[:, :, None]).astype(jnp.bfloat16)
        updated = through[:, None, None] * memory + jnp.einsum('shd,she->hde', key_scaled.astype(jnp.float32), value_wide, precision=highest)
        return (updated, (within + carried, memory))
    initial = jnp.zeros((HEADS, HEAD_DIM, HEAD_DIM), jnp.float32)
    _, (attended, incoming_state) = lax.scan(forward_block, initial, (query_blocks, key_blocks, value_blocks, decays, start_marks))
    attended = attended.reshape(TOKENS, HEADS * HEAD_DIM)
    squares = lax.optimization_barrier(jnp.mean(attended * attended, axis=1))
    spread_rms = jnp.sqrt(squares + epsilon)
    normed = attended / spread_rms[:, None]
    opening = jax.nn.sigmoid(gate_logits.astype(jnp.float32))
    upstream = grad_out.astype(jnp.float32)
    grad_gate = (upstream * norm_gain[None, :] * normed * opening * (1.0 - opening)).astype(jnp.bfloat16)
    dnormed = upstream * norm_gain[None, :] * opening
    projection = lax.optimization_barrier(jnp.mean(dnormed * normed, axis=1))
    grad_attn = ((dnormed - normed * projection[:, None]) / spread_rms[:, None]).astype(jnp.bfloat16)
    grad_blocks = shaped(grad_attn)

    def backward_block(memory, pieces):
        query_here, key_here, value_here, decay_here, mark_here, grad_here, entering_here = pieces
        multiplier, inward, outward, through = factors_of(decay_here, mark_here)
        query_wide = query_here.astype(jnp.float32)
        key_wide = key_here.astype(jnp.float32)
        value_wide = value_here.astype(jnp.float32)
        grad_wide = grad_here.astype(jnp.float32)
        scores = jnp.einsum('thd,shd->hts', query_wide, key_wide, precision=highest)
        mixing = (multiplier * scores).astype(jnp.bfloat16).astype(jnp.float32)
        scores_gradient = jnp.einsum('the,she->hts', grad_wide, value_wide, precision=highest)
        grad_mixing = (multiplier * scores_gradient).astype(jnp.bfloat16).astype(jnp.float32)
        grad_query = jnp.einsum('hts,shd->thd', grad_mixing, key_wide, precision=highest) + jnp.einsum('the,hde->thd', grad_wide, entering_here, precision=highest) * inward[:, :, None]
        grad_key = jnp.einsum('hts,thd->shd', grad_mixing, query_wide, precision=highest) + jnp.einsum('she,hde->shd', value_wide, memory, precision=highest) * outward[:, :, None]
        grad_value = jnp.einsum('hts,the->she', mixing, grad_wide, precision=highest) + jnp.einsum('shd,hde->she', key_wide, memory, precision=highest) * outward[:, :, None]
        query_scaled = (query_wide * inward[:, :, None]).astype(jnp.bfloat16)
        updated = through[:, None, None] * memory + jnp.einsum('thd,the->hde', query_scaled.astype(jnp.float32), grad_wide, precision=highest)
        return (updated, (grad_query.astype(jnp.bfloat16), grad_key.astype(jnp.bfloat16), grad_value.astype(jnp.bfloat16)))
    _, (grad_query, grad_key, grad_value) = lax.scan(backward_block, initial, (query_blocks, key_blocks, value_blocks, decays, start_marks, grad_blocks, incoming_state), reverse=True)
    width = HEADS * HEAD_DIM
    return (grad_query.reshape(TOKENS, width), grad_key.reshape(TOKENS, width), grad_value.reshape(TOKENS, width), grad_gate)
```

```python
import functools

import jax
import jax.numpy as jnp
from jax import lax
from jax.experimental import pallas as pl
from jax.experimental.pallas import tpu as pltpu
from jax.sharding import PartitionSpec as P

HEAD_DIM = 128
TOK = 256
HALF = 4
EPSILON = 1e-06
HIGHEST = lax.Precision.HIGHEST
F32 = jnp.float32
BF16 = jnp.bfloat16
NEG = -1e30


def dot(a, b, ca, cb, precision=None):
    return lax.dot_general(
        a, b, (((ca,), (cb,)), ((), ())), precision=precision, preferred_element_type=F32
    )


def split(a):
    high = a.astype(BF16)
    return high, (a - high.astype(F32)).astype(BF16)


def call(kernel, outs, n_smem, *args, **kw):
    smem = pl.BlockSpec(memory_space=pltpu.SMEM)
    vmem = pl.BlockSpec(memory_space=pltpu.VMEM)
    return pl.pallas_call(
        kernel,
        out_shape=[jax.ShapeDtypeStruct(s, d) for s, d in outs],
        in_specs=[smem] * n_smem + [vmem] * (len(args) - n_smem),
        out_specs=[vmem] * len(outs),
        compiler_params=pltpu.CompilerParams(vmem_limit_bytes=24 * 1024 * 1024),
        **kw,
    )(*args)


def cols(core, slot):
    return pl.ds(pl.multiple_of(((slot + HALF * core) % 8) * HEAD_DIM, HEAD_DIM), HEAD_DIM)


def here(slot):
    return slice(slot * HEAD_DIM, (slot + 1) * HEAD_DIM)


def first_start(starts):
    return starts[0, 0]


def last_start(starts, place):
    latest = jnp.full_like(place, -1)
    for j in range(4):
        latest = jnp.maximum(latest, jnp.where(starts[0, j] <= place, starts[0, j], -1))
    return latest


def last_of_block(starts):
    latest = jnp.int32(-1)
    for j in range(4):
        latest = jnp.maximum(latest, jnp.where(starts[0, j] < TOK, starts[0, j], -1))
    return latest


def outward_of(starts, summed_col):
    place = lax.broadcasted_iota(jnp.int32, summed_col.shape, 0)
    spread = summed_col[TOK - 1 : TOK, :] - summed_col
    return jnp.exp(jnp.where(place >= last_of_block(starts), spread, NEG))


def inward_of(starts, summed_col):
    place = lax.broadcasted_iota(jnp.int32, summed_col.shape, 0)
    return jnp.exp(jnp.where(place < first_start(starts), summed_col, NEG))


def through_rows(starts, summed_col, slots):
    last = jnp.where(last_of_block(starts) < 0, summed_col[TOK - 1 : TOK, :], NEG)
    factor = jnp.exp(last)
    return [jnp.broadcast_to(factor[:, s : s + 1], (1, HEAD_DIM)) for s in slots]


def weight_of(starts, summed_row, summed_col, slot):
    t = lax.broadcasted_iota(jnp.int32, (TOK, TOK), 0)
    s = lax.broadcasted_iota(jnp.int32, (TOK, TOK), 1)
    keep = jnp.logical_and(s <= t, s >= last_start(starts, t))
    spread = summed_col[:, slot : slot + 1] - summed_row[slot : slot + 1, :]
    return jnp.exp(jnp.where(keep, spread, NEG))


def state_of(left, scale, right):
    scaled = (left.astype(F32) * scale).astype(BF16)
    return dot(scaled, right, 0, 0)


def k_first(core_ref, starts, decay, k, v, send, rows, summed_cols):
    core = core_ref[0]
    d = decay[...]
    d = jnp.where(core == 0, d, jnp.concatenate([d[HALF:], d[:HALF]], axis=0))
    a = lax.broadcasted_iota(jnp.int32, (TOK, TOK), 0)
    b = lax.broadcasted_iota(jnp.int32, (TOK, TOK), 1)
    rows[...] = dot(d, (a <= b).astype(F32), 1, 0, HIGHEST)
    col = dot((b <= a).astype(F32), d, 1, 1, HIGHEST)
    summed_cols[...] = col
    outward = outward_of(starts, col)
    for i in range(HALF):
        at = cols(core, HALF + i)
        send[i * 128 : (i + 1) * 128, :] = state_of(k[:, at], outward[:, HALF + i : HALF + i + 1], v[:, at])
    send[512:520, :] = jnp.concatenate(
        through_rows(starts, col, range(HALF, 8)) + [jnp.zeros((HALF, HEAD_DIM), F32)], axis=0
    )


def k_local(core_ref, starts, rows, summed_cols, q, k, v, mine, within):
    core = core_ref[0]
    row, col = rows[...], summed_cols[...]
    outward = outward_of(starts, col)
    for i in range(HALF):
        at = cols(core, i)
        mine[i * 128 : (i + 1) * 128, :] = state_of(k[:, at], outward[:, i : i + 1], v[:, at])
    mine[512:520, :] = jnp.concatenate(
        through_rows(starts, col, range(HALF)) + [jnp.zeros((HALF, HEAD_DIM), F32)], axis=0
    )
    for slot in range(8):
        at = cols(core, slot)
        scores = dot(q[:, at], k[:, at], 1, 1)
        mixing = (weight_of(starts, row, col, slot) * scores).astype(BF16)
        within[:, here(slot)] = dot(mixing, v[:, at], 1, 0)


def k_pack(core_ref, mine, other, out):
    first = core_ref[0] == 0
    for i in range(HALF):
        at = slice(i * 128, (i + 1) * 128)
        g_mine, g_other = mine[512 + i : 513 + i, :], other[512 + i : 513 + i, :]
        s_mine, s_other = mine[at, :], other[at, :]
        state = jnp.where(first, s_mine * g_other + s_other, s_other * g_mine + s_mine)
        for j in range(8):
            out[8 * i + j, 0:16, :] = state[16 * j : 16 * (j + 1), :]
            out[8 * i + j, 16:24, :] = jnp.broadcast_to(g_mine * g_other, (8, HEAD_DIM))


def k_scan(pieces, out):
    state = jnp.zeros((16, HEAD_DIM), F32)
    for i in range(32):
        out[i] = state
        state = state * pieces[i, 16:17, :] + pieces[i, 0:16, :]


def k_scan_back(pieces, factors, out):
    state = jnp.zeros((16, HEAD_DIM), F32)
    for i in reversed(range(32)):
        out[i] = state
        state = state * factors[i, 16:17, :] + pieces[i]


def k_enter(core_ref, entering, mine, other, e_mine, e_send):
    first = core_ref[0] == 0
    for i in range(HALF):
        at = slice(i * 128, (i + 1) * 128)
        g0 = jnp.where(first, mine[512 + i : 513 + i, :], other[512 + i : 513 + i, :])
        s0 = jnp.where(first, mine[at, :], other[at, :])
        e0 = entering[at, :]
        e1 = e0 * g0 + s0
        e_mine[at, :] = jnp.where(first, e0, e1)
        e_send[at, :] = jnp.where(first, e1, e0)


def k_attend(core_ref, starts, summed_cols, q, within, e_mine, out):
    core = core_ref[0]
    inward = inward_of(starts, summed_cols[...])
    for i in range(HALF):
        high, low = split(e_mine[i * 128 : (i + 1) * 128, :])
        query = q[:, cols(core, i)]
        carried = dot(query, high, 1, 0) + dot(query, low, 1, 0)
        out[:, here(i)] = within[:, here(i)] + carried * inward[:, i : i + 1]


def k_sums(core_ref, starts, summed_cols, q, within, e_other, att_mine, gate, gain, up, att_other, sums):
    core = core_ref[0]
    inward = inward_of(starts, summed_cols[...])
    squares = jnp.zeros((TOK, HEAD_DIM), F32)
    products = jnp.zeros((TOK, HEAD_DIM), F32)
    for slot in range(8):
        at = cols(core, slot)
        if slot < HALF:
            att = att_mine[:, here(slot)]
        else:
            i = slot - HALF
            high, low = split(e_other[i * 128 : (i + 1) * 128, :])
            query = q[:, at]
            carried = dot(query, high, 1, 0) + dot(query, low, 1, 0)
            att = within[:, here(slot)] + carried * inward[:, slot : slot + 1]
            att_other[:, here(i)] = att
        dnormed = up[:, at].astype(F32) * gain[:, at] * jax.nn.sigmoid(gate[:, at].astype(F32))
        squares += att * att
        products += dnormed * att
    ones = jnp.ones((8, HEAD_DIM), F32)
    line = lax.broadcasted_iota(jnp.int32, (8, TOK), 0)
    both = jnp.where(line < 4, dot(ones, squares, 1, 1, HIGHEST), dot(ones, products, 1, 1, HIGHEST))
    for j in range(4):
        sums[j] = both


def k_grad(core_ref, starts, summed_cols, sums, att_mine, att_other, gate, gain, up, q, grad, send, grad_gate, *, features):
    core = core_ref[0]
    inward = inward_of(starts, summed_cols[...])
    total = sums[0] + sums[1] + sums[2] + sums[3]
    line = lax.broadcasted_iota(jnp.int32, (8, HEAD_DIM), 0)
    squares = dot(total, (line == 0).astype(F32), 0, 0, HIGHEST)
    products = dot(total, (line == 4).astype(F32), 0, 0, HIGHEST)
    inverse = 1.0 / jnp.sqrt(squares / features + EPSILON)
    projection = products * inverse / features
    for slot in reversed(range(8)):
        at = cols(core, slot)
        att = att_mine[:, here(slot)] if slot < HALF else att_other[:, here(slot - HALF)]
        opening = jax.nn.sigmoid(gate[:, at].astype(F32))
        dnormed = up[:, at].astype(F32) * gain[:, at] * opening
        normed = att * inverse
        grad_gate[:, at] = (dnormed * normed * (1.0 - opening)).astype(BF16)
        value = ((dnormed - normed * projection) * inverse).astype(BF16)
        grad[:, here(slot)] = value
        if slot >= HALF:
            i = slot - HALF
            send[i * 128 : (i + 1) * 128, :] = state_of(q[:, at], inward[:, slot : slot + 1], value)


def k_back(core_ref, starts, rows, summed_cols, q, k, v, grad, e_mine, e_other, mine, gq, gk, gv):
    core = core_ref[0]
    row, col = rows[...], summed_cols[...]
    inward = inward_of(starts, col)
    for slot in range(8):
        at = cols(core, slot)
        query, key, value, upstream = q[:, at], k[:, at], v[:, at], grad[:, here(slot)]
        i = slot % HALF
        if slot < HALF:
            mine[i * 128 : (i + 1) * 128, :] = state_of(query, inward[:, slot : slot + 1], upstream)
        weight = weight_of(starts, row, col, slot)
        mixing = (weight * dot(query, key, 1, 1)).astype(BF16)
        grad_mixing = (weight * dot(upstream, value, 1, 1)).astype(BF16)
        state = (e_mine if slot < HALF else e_other)[i * 128 : (i + 1) * 128, :]
        high, low = split(state)
        carried = dot(upstream, high, 1, 1) + dot(upstream, low, 1, 1)
        gq[:, at] = (dot(grad_mixing, key, 1, 0) + carried * inward[:, slot : slot + 1]).astype(BF16)
        gk[:, here(slot)] = dot(grad_mixing, query, 0, 0)
        gv[:, here(slot)] = dot(mixing, upstream, 0, 0)


def k_pack_back(core_ref, mine, other, s_mine, s_other, out):
    first = core_ref[0] == 0
    for i in range(HALF):
        at = slice(i * 128, (i + 1) * 128)
        g0 = jnp.where(first, s_mine[512 + i : 513 + i, :], s_other[512 + i : 513 + i, :])
        b_mine, b_other = mine[at, :], other[at, :]
        state = jnp.where(first, b_mine + g0 * b_other, b_other + g0 * b_mine)
        for j in range(8):
            out[8 * i + j] = state[16 * j : 16 * (j + 1), :]


def k_leave(core_ref, leaving, mine, other, s_mine, s_other, l_mine, l_send):
    first = core_ref[0] == 0
    for i in range(HALF):
        at = slice(i * 128, (i + 1) * 128)
        g1 = jnp.where(first, s_other[512 + i : 513 + i, :], s_mine[512 + i : 513 + i, :])
        b1 = jnp.where(first, other[at, :], mine[at, :])
        l1 = leaving[at, :]
        l0 = l1 * g1 + b1
        l_mine[at, :] = jnp.where(first, l0, l1)
        l_send[at, :] = jnp.where(first, l1, l0)


def finish(core, slot, state, outward, k, v, gk, gv):
    at = cols(core, slot)
    high, low = split(state)
    value, key = v[:, at], k[:, at]
    scale = outward[:, slot : slot + 1]
    to_key = dot(value, high, 1, 1) + dot(value, low, 1, 1)
    to_value = dot(key, high, 1, 0) + dot(key, low, 1, 0)
    return (
        (gk[:, here(slot)] + to_key * scale).astype(BF16),
        (gv[:, here(slot)] + to_value * scale).astype(BF16),
    )


def k_end_mine(core_ref, starts, summed_cols, k, v, gk, gv, l_mine, out_k, out_v):
    core = core_ref[0]
    outward = outward_of(starts, summed_cols[...])
    for i in range(HALF):
        state = l_mine[i * 128 : (i + 1) * 128, :]
        out_k[:, here(i)], out_v[:, here(i)] = finish(core, i, state, outward, k, v, gk, gv)


def k_end(core_ref, starts, summed_cols, k, v, gk, gv, l_other, k_mine, v_mine, out_k, out_v):
    core = core_ref[0]
    outward = outward_of(starts, summed_cols[...])
    for i in range(HALF):
        at = cols(core, i)
        out_k[:, at] = k_mine[:, here(i)]
        out_v[:, at] = v_mine[:, here(i)]
    for i in range(HALF):
        at = cols(core, HALF + i)
        state = l_other[i * 128 : (i + 1) * 128, :]
        out_k[:, at], out_v[:, at] = finish(core, HALF + i, state, outward, k, v, gk, gv)


def local(q, k, v, decay, starts, gate, gain, up):
    places = lax.axis_size("seq")
    swap = [(i, i ^ 1) for i in range(places)]
    groups = [list(range(c, places, 2)) for c in range(2)]
    core = (lax.axis_index("seq") % 2).astype(jnp.int32).reshape(1)
    features = q.shape[1] * lax.axis_size("head")
    gain = gain.reshape(1, -1)
    wide, half = (TOK, 1024), (TOK, 512)
    state, state_g = (512, HEAD_DIM), (520, HEAD_DIM)

    def trade(a):
        return lax.all_to_all(a, "seq", 0, 0, axis_index_groups=groups)

    send, rows, summed = call(
        k_first, [(state_g, F32), ((8, TOK), F32), ((TOK, 8), F32)], 2, core, starts, decay, k, v
    )
    s_other = lax.ppermute(send, "seq", swap)
    s_mine, within = call(k_local, [(state_g, F32), (wide, F32)], 2, core, starts, rows, summed, q, k, v)
    (pieces,) = call(k_pack, [((32, 24, HEAD_DIM), F32)], 1, core, s_mine, s_other)
    pieces = trade(pieces)
    (entering,) = call(k_scan, [((32, 16, HEAD_DIM), F32)], 0, pieces)
    entering = trade(entering).reshape(state)
    e_mine, e_send = call(k_enter, [(state, F32)] * 2, 1, core, entering, s_mine, s_other)
    e_other = lax.ppermute(e_send, "seq", swap)
    (att_mine,) = call(k_attend, [(half, F32)], 2, core, starts, summed, q, within, e_mine)
    att_other, sums = call(
        k_sums,
        [(half, F32), ((4, 8, TOK), F32)],
        2, core, starts, summed, q, within, e_other, att_mine, gate, gain, up,
    )
    sums = lax.all_to_all(sums, "head", 0, 0)
    grad, b_send, grad_gate = call(
        functools.partial(k_grad, features=float(features)),
        [(wide, BF16), (state, F32), (wide, BF16)],
        2, core, starts, summed, sums, att_mine, att_other, gate, gain, up, q,
    )
    b_other = lax.ppermute(b_send, "seq", swap)
    b_mine, gq, gk, gv = call(
        k_back,
        [(state, F32), (wide, BF16), (wide, F32), (wide, F32)],
        2, core, starts, rows, summed, q, k, v, grad, e_mine, e_other,
    )
    (back,) = call(k_pack_back, [((32, 16, HEAD_DIM), F32)], 1, core, b_mine, b_other, s_mine, s_other)
    back = trade(back)
    (leaving,) = call(k_scan_back, [((32, 16, HEAD_DIM), F32)], 0, back, pieces)
    leaving = trade(leaving).reshape(state)
    l_mine, l_send = call(k_leave, [(state, F32)] * 2, 1, core, leaving, b_mine, b_other, s_mine, s_other)
    l_other = lax.ppermute(l_send, "seq", swap)
    k_mine, v_mine = call(k_end_mine, [(half, BF16)] * 2, 2, core, starts, summed, k, v, gk, gv, l_mine)
    grad_key, grad_value = call(
        k_end, [(wide, BF16)] * 2, 2, core, starts, summed, k, v, gk, gv, l_other, k_mine, v_mine
    )
    return gq, grad_key, grad_value, grad_gate


def solution(mesh):
    token = P("seq", "head")
    return jax.shard_map(
        local,
        mesh=mesh,
        in_specs=(token, token, token, P("head", "seq"), P("seq", None), token, P("head"), token),
        out_specs=(token,) * 4,
        check_vma=False,
    )
```

```python
import functools

import jax
import jax.numpy as jnp
from jax import lax
from jax.experimental import pallas as pl
from jax.experimental.pallas import tpu as pltpu
from jax.sharding import PartitionSpec as P

HEAD_DIM = 128
TOK = 256
HALF = 4
EPSILON = 1e-06
F32 = jnp.float32
BF16 = jnp.bfloat16
NEG = -1e30


def dot(a, b, ca, cb):
    return lax.dot_general(a, b, (((ca,), (cb,)), ((), ())), preferred_element_type=F32)


def parts(a, count):
    out = []
    for _ in range(count):
        out.append(a.astype(BF16))
        a = a - out[-1].astype(F32)
    return out


def wide_dot(a, state, axis):
    return dot(jnp.concatenate([a, a], axis=1), jnp.concatenate(parts(state, 2), axis=axis), 1, axis)


def call(kernel, outs, n_smem, *args, hbm=(), hbm_out=(), scratch=(), vmem_mib=24, **kw):
    smem = pl.BlockSpec(memory_space=pltpu.SMEM)
    vmem = pl.BlockSpec(memory_space=pltpu.VMEM)
    far = pl.BlockSpec(memory_space=pltpu.HBM)
    return pl.pallas_call(
        kernel,
        out_shape=[jax.ShapeDtypeStruct(s, d) for s, d in outs],
        in_specs=[smem] * n_smem + [far if n in hbm else vmem for n in range(n_smem, len(args))],
        out_specs=[far if n in hbm_out else vmem for n in range(len(outs))],
        scratch_shapes=list(scratch),
        compiler_params=pltpu.CompilerParams(vmem_limit_bytes=int(vmem_mib * 1024 * 1024)),
        **kw,
    )(*args)


def cols(core, slot):
    return pl.ds(pl.multiple_of(((slot + HALF * core) % 8) * HEAD_DIM, HEAD_DIM), HEAD_DIM)


def half_cols(half):
    width = HALF * HEAD_DIM
    return pl.ds(pl.multiple_of(half * width, width), width)


def here(slot):
    return slice(slot * HEAD_DIM, (slot + 1) * HEAD_DIM)


def spread(lines, count):
    n = lines.shape[0]
    shape = (count * n, n * HEAD_DIM)
    line = lax.broadcasted_iota(jnp.int32, shape, 0) % n
    head = lax.broadcasted_iota(jnp.int32, shape, 1) // HEAD_DIM
    pick = (line == head).astype(F32).astype(BF16)
    return dot(jnp.concatenate(parts(lines, count), axis=0), pick, 0, 0)


def latest_of(rows):
    return rows[8:9, :]


def outward_of(rows, slots):
    row, latest = rows[slots, :], latest_of(rows)
    place = lax.broadcasted_iota(jnp.int32, row.shape, 1).astype(F32)
    kept = place >= latest[:, TOK - 1 : TOK]
    return jnp.exp(jnp.where(kept, row[:, TOK - 1 : TOK] - row, NEG))


def inward_of(rows):
    return jnp.exp(jnp.where(latest_of(rows) < 0, rows[0:8, :], NEG))


def through_of(rows):
    last = jnp.where(latest_of(rows)[:, TOK - 1 : TOK] < 0, rows[0:8, TOK - 1 : TOK], NEG)
    return jnp.broadcast_to(jnp.exp(last), (8, HEAD_DIM))


def state_of(left, scale, right):
    return dot((left.astype(F32) * scale).astype(BF16), right, 0, 0)


def fetch(pairs, sems):
    copies = [pltpu.make_async_copy(src, dst, sems.at[n]) for n, (src, dst) in enumerate(pairs)]
    for copy in copies:
        copy.start()
    return copies


def k_first(core_ref, aux, k, v, send, rows, kbuf, vbuf, sems):
    core = core_ref[0]
    there = half_cols(1 - core)
    copies = fetch([(k.at[:, there], kbuf), (v.at[:, there], vbuf)], sems)
    a = lax.broadcasted_iota(jnp.int32, (TOK, TOK), 0)
    b = lax.broadcasted_iota(jnp.int32, (TOK, TOK), 1)
    d = aux[0:8, :]
    d = jnp.where(core == 0, d, jnp.concatenate([d[HALF:], d[:HALF]], axis=0))
    sums = dot(jnp.concatenate(parts(d, 3), axis=0), (a <= b).astype(BF16), 1, 0)
    rows[0:8, :] = sums[0:8] + sums[8:16] + sums[16:24]
    place = lax.broadcasted_iota(jnp.int32, (1, TOK), 1).astype(F32)
    latest = jnp.full((1, TOK), -1.0, F32)
    for j in range(4):
        begin = aux[8:9, j : j + 1]
        latest = jnp.maximum(latest, jnp.where(begin <= place, begin, -1.0))
    rows[8:16, :] = jnp.broadcast_to(latest, (8, TOK))
    outward = spread(outward_of(rows, slice(HALF, 8)), 2)
    through = through_of(rows)
    send[512:520, :] = jnp.concatenate([through[HALF:8], through[0:HALF]], axis=0)
    for copy in copies:
        copy.wait()
    for i in range(HALF):
        send[i * 128 : (i + 1) * 128, :] = state_of(kbuf[:, here(i)], outward[:, here(i)], vbuf[:, here(i)])


def mixed(weight, query, key, value):
    return dot((weight * dot(query, key, 1, 1)).astype(BF16), value, 1, 0)


def biases(rows):
    latest = spread(latest_of(rows), 1)
    t = lax.broadcasted_iota(jnp.int32, (TOK, HEAD_DIM), 0)
    s = lax.broadcasted_iota(jnp.int32, (TOK, HEAD_DIM), 1)
    out = []
    for part in range(2):
        place = s + part * HEAD_DIM
        out.append(jnp.where(jnp.logical_and(place <= t, place.astype(F32) >= latest), 0.0, NEG))
    return out


def weight_of(rows, column, bias, slot):
    line = rows[slot : slot + 1, :]
    return jnp.concatenate(
        [jnp.exp(column - line[:, here(part)] + bias[part]) for part in range(2)], axis=1
    )


def k_local(core_ref, rows, q, k, v, mine, within, qbuf, kbuf, vbuf, sems):
    core = core_ref[0]
    there = half_cols(core)
    copies = fetch([(k.at[:, there], kbuf), (v.at[:, there], vbuf), (q.at[:, there], qbuf)], sems)
    columns = spread(rows[0:HALF, :], 3)
    bias = biases(rows)
    outward = spread(outward_of(rows, slice(0, HALF)), 2)
    mine[512:520, :] = through_of(rows)
    copies[0].wait()
    copies[1].wait()
    for i in range(HALF):
        mine[i * 128 : (i + 1) * 128, :] = state_of(kbuf[:, here(i)], outward[:, here(i)], vbuf[:, here(i)])
    copies[2].wait()
    for i in range(HALF):
        weight = weight_of(rows, columns[:, here(i)], bias, i)
        within[:, here(i)] = mixed(weight, qbuf[:, here(i)], kbuf[:, here(i)], vbuf[:, here(i)])


def k_pack(core_ref, mine, other, out):
    first = core_ref[0] == 0
    for i in range(HALF):
        at = slice(i * 128, (i + 1) * 128)
        g_mine, g_other = mine[512 + i : 513 + i, :], other[512 + i : 513 + i, :]
        s_mine, s_other = mine[at, :], other[at, :]
        state = jnp.where(first, s_mine * g_other + s_other, s_other * g_mine + s_mine)
        for j in range(8):
            base = 17 * (8 * i + j)
            out[base : base + 16, :] = state[16 * j : 16 * (j + 1), :]
            out[base + 16 : base + 17, :] = g_mine * g_other


def k_scan(pieces, out):
    state = jnp.zeros((16, HEAD_DIM), F32)
    for i in range(32):
        out[i] = state
        state = state * pieces[17 * i + 16 : 17 * i + 17, :] + pieces[17 * i : 17 * i + 16, :]


def k_scan_back(pieces, factors, out):
    state = jnp.zeros((16, HEAD_DIM), F32)
    for i in reversed(range(32)):
        out[i] = state
        state = state * factors[17 * i + 16 : 17 * i + 17, :] + pieces[i]


def k_enter(core_ref, entering, mine, other, e_mine, e_send):
    first = core_ref[0] == 0
    for i in range(HALF):
        at = slice(i * 128, (i + 1) * 128)
        g0 = jnp.where(first, mine[512 + i : 513 + i, :], other[512 + i : 513 + i, :])
        s0 = jnp.where(first, mine[at, :], other[at, :])
        e0 = entering[at, :]
        e1 = e0 * g0 + s0
        e_mine[at, :] = jnp.where(first, e0, e1)
        e_send[at, :] = jnp.where(first, e1, e0)


def k_attend(
    core_ref, rows, q, k, v, within, e_mine, gate, gain, up,
    att_mine, dnormed, within_other, part, inward,
):
    core = core_ref[0]
    inward[...] = spread(inward_of(rows), 2)
    columns = spread(rows[HALF:8, :], 3)
    bias = biases(rows)
    squares = jnp.zeros((TOK, HEAD_DIM), F32)
    products = jnp.zeros((TOK, HEAD_DIM), F32)
    for slot in range(8):
        at = cols(core, slot)
        dn = up[:, at].astype(F32) * gain[:, at] * jax.nn.sigmoid(gate[:, at].astype(F32))
        dnormed[:, here(slot)] = dn
        if slot < HALF:
            carried = wide_dot(q[:, at], e_mine[slot * 128 : (slot + 1) * 128, :], 0)
            att = within[:, here(slot)] + carried * inward[:, here(slot)]
            att_mine[:, here(slot)] = att
            squares += att * att
            products += dn * att
        else:
            weight = weight_of(rows, columns[:, here(slot - HALF)], bias, slot)
            within_other[:, here(slot - HALF)] = mixed(weight, q[:, at], k[:, at], v[:, at])
    part[0] = squares
    part[1] = products


def k_sums(core_ref, q, within, inward, e_other, part, dnormed, att_other, sums):
    core = core_ref[0]
    squares, products = part[0], part[1]
    for i in range(HALF):
        slot = HALF + i
        carried = wide_dot(q[:, cols(core, slot)], e_other[i * 128 : (i + 1) * 128, :], 0)
        att = within[:, here(i)] + carried * inward[:, here(slot)]
        att_other[:, here(i)] = att
        squares += att * att
        products += dnormed[:, here(slot)] * att
    ones = jnp.ones((8, 2 * HEAD_DIM), BF16)
    line = lax.broadcasted_iota(jnp.int32, (8, TOK), 0)
    sums[...] = jnp.where(
        line < 4,
        dot(ones, jnp.concatenate(parts(squares, 2), axis=1), 1, 1),
        dot(ones, jnp.concatenate(parts(products, 2), axis=1), 1, 1),
    )


def k_mid(
    core_ref, rows, q, k, gate, att_mine, att_other, dnormed, inward,
    weights, turned, mixings, factor, scaled,
):
    core = core_ref[0]
    latest = latest_of(rows)
    columns = spread(rows[0:8, :], 3)
    biased = biases(rows)
    for slot in range(8):
        weights[slot] = weight_of(rows, columns[:, here(slot)], biased, slot)
    s = lax.broadcasted_iota(jnp.int32, (TOK, HEAD_DIM), 0)
    t = lax.broadcasted_iota(jnp.int32, (TOK, HEAD_DIM), 1)
    for part in range(2):
        at = here(part)
        kept = jnp.logical_and(s <= t + part * HEAD_DIM, s.astype(F32) >= latest[:, at])
        bias = jnp.where(kept, 0.0, NEG)
        for slot in range(8):
            turned[slot, :, at] = jnp.exp(rows[slot : slot + 1, at] - columns[:, here(slot)] + bias)
    for slot in reversed(range(8)):
        at = cols(core, slot)
        i = slot % HALF
        query = q[:, at]
        scaled[slot] = (query.astype(F32) * inward[:, here(slot)]).astype(BF16).T
        mixings[slot] = (turned[slot] * dot(k[:, at], query, 1, 1)).astype(BF16)
        att = (att_mine if slot < HALF else att_other)[:, here(i)]
        opening = jax.nn.sigmoid(gate[:, at].astype(F32))
        factor[:, here(slot)] = dnormed[:, here(slot)] * att * (1.0 - opening)


def grad_of(att, dnormed, inverse, projection):
    return ((dnormed - att * inverse * projection) * inverse).astype(BF16)


def k_grad(sums0, sums1, sums2, sums3, att, dnormed, scaled, grad, send, inverses, projections, *, features):
    total = sums0[...] + sums1[...] + sums2[...] + sums3[...]
    inverse = 1.0 / jnp.sqrt(total[0:1] / features + EPSILON)
    both = spread(jnp.concatenate([inverse, total[4:5] * inverse / features], axis=0), 3)
    inverse, projection = both[:, :HEAD_DIM], both[:, HEAD_DIM:]
    for i in range(HALF):
        slot = HALF + i
        value = grad_of(att[:, here(i)], dnormed[:, here(slot)], inverse, projection)
        grad[:, here(i)] = value
        send[i * 128 : (i + 1) * 128, :] = dot(scaled[slot], value, 1, 0)
    inverses[...] = inverse
    projections[...] = projection


def k_back(
    core_ref, inverses, projections, att_mine, dnormed, grad_other, k, v,
    weights, turned, factor, inward, scaled, e_mine, e_other,
    mine, grad_mine, gq, gate_out, mixed_back,
):
    core = core_ref[0]
    inverse, projection = inverses[...], projections[...]
    for slot in range(8):
        at = cols(core, slot)
        i = slot % HALF
        key, value = k[:, at], v[:, at]
        if slot < HALF:
            upstream = grad_of(att_mine[:, here(i)], dnormed[:, here(slot)], inverse, projection)
            grad_mine[:, here(i)] = upstream
            mine[i * 128 : (i + 1) * 128, :] = dot(scaled[slot], upstream, 1, 0)
        else:
            upstream = grad_other[:, here(i)]
        grad_mixing = (weights[slot] * dot(upstream, value, 1, 1)).astype(BF16)
        mixed_back[slot] = (turned[slot] * dot(value, upstream, 1, 1)).astype(BF16)
        state = (e_mine if slot < HALF else e_other)[i * 128 : (i + 1) * 128, :]
        carried = wide_dot(upstream, state, 1)
        gq[:, at] = (dot(grad_mixing, key, 1, 0) + carried * inward[:, here(slot)]).astype(BF16)
        gate_out[:, at] = (factor[:, here(slot)] * inverse).astype(BF16)


def k_pack_back(core_ref, mine, other, s_mine, s_other, out):
    first = core_ref[0] == 0
    for i in range(HALF):
        at = slice(i * 128, (i + 1) * 128)
        g0 = jnp.where(first, s_mine[512 + i : 513 + i, :], s_other[512 + i : 513 + i, :])
        b_mine, b_other = mine[at, :], other[at, :]
        state = jnp.where(first, b_mine + g0 * b_other, b_other + g0 * b_mine)
        for j in range(8):
            out[8 * i + j] = state[16 * j : 16 * (j + 1), :]


def k_leave(core_ref, leaving, mine, other, s_mine, s_other, l_mine, l_send):
    first = core_ref[0] == 0
    for i in range(HALF):
        at = slice(i * 128, (i + 1) * 128)
        g1 = jnp.where(first, s_other[512 + i : 513 + i, :], s_mine[512 + i : 513 + i, :])
        b1 = jnp.where(first, other[at, :], mine[at, :])
        l1 = leaving[at, :]
        l0 = l1 * g1 + b1
        l_mine[at, :] = jnp.where(first, l0, l1)
        l_send[at, :] = jnp.where(first, l1, l0)


def finish(state, scale, key, value, part_k, part_v):
    to_key = wide_dot(value, state, 1)
    to_value = wide_dot(key, state, 0)
    return (part_k + to_key * scale).astype(BF16), (part_v + to_value * scale).astype(BF16)


def k_end_mine(
    core_ref, rows, q, k, v, grad_mine, grad_other, mixed_back, mixings, l_mine, gq, gate_in,
    part_k, part_v, outward_other, k_mine, v_mine, out_q, out_gate, sems,
):
    core = core_ref[0]
    copies = fetch([(gq, out_q), (gate_in, out_gate)], sems)
    outward = spread(outward_of(rows, slice(0, 8)), 2)
    outward_other[...] = outward[:, 512:]
    for slot in range(8):
        i = slot % HALF
        at = cols(core, slot)
        upstream = (grad_mine if slot < HALF else grad_other)[:, here(i)]
        to_key = dot(mixed_back[slot], q[:, at], 1, 0)
        to_value = dot(mixings[slot], upstream, 1, 0)
        if slot < HALF:
            state = l_mine[i * 128 : (i + 1) * 128, :]
            k_mine[:, here(i)], v_mine[:, here(i)] = finish(
                state, outward[:, here(slot)], k[:, at], v[:, at], to_key, to_value
            )
        else:
            part_k[:, here(i)] = to_key
            part_v[:, here(i)] = to_value
    for copy in copies:
        copy.wait()


def k_end(
    core_ref, outward, k, v, part_k, part_v, l_other, k_mine, v_mine,
    out_k, out_v, kbuf, vbuf, sems,
):
    core = core_ref[0]
    there = half_cols(core)
    copies = fetch([(k_mine, out_k.at[:, there]), (v_mine, out_v.at[:, there])], sems)
    for i in range(HALF):
        slot = HALF + i
        at = cols(core, slot)
        state = l_other[i * 128 : (i + 1) * 128, :]
        kbuf[:, here(i)], vbuf[:, here(i)] = finish(
            state, outward[:, here(i)], k[:, at], v[:, at], part_k[:, here(i)], part_v[:, here(i)]
        )
        for n, (buf, out) in enumerate(((kbuf, out_k), (vbuf, out_v))):
            copies.append(pltpu.make_async_copy(buf.at[:, here(i)], out.at[:, at], sems.at[2 + 2 * i + n]))
            copies[-1].start()
    for copy in copies:
        copy.wait()


def local(q, k, v, decay, starts, gate, gain, up):
    places = lax.axis_size("seq")
    swap = [(i, i ^ 1) for i in range(places)]
    groups = [list(range(c, places, 2)) for c in range(2)]
    core = (lax.axis_index("seq") % 2).astype(jnp.int32).reshape(1)
    heads = lax.axis_size("head")
    features = q.shape[1] * heads
    gain = gain.reshape(1, -1)
    wide, half = (TOK, 1024), (TOK, 512)
    state, state_g = (512, HEAD_DIM), (520, HEAD_DIM)
    square = (8, TOK, TOK)
    buffer = pltpu.VMEM(half, BF16)

    def trade(a):
        return lax.all_to_all(a, "seq", 0, 0, axis_index_groups=groups)

    def around(a, step):
        return lax.ppermute(a, "head", [(i, (i + step) % heads) for i in range(heads)])

    begins = jnp.pad(starts.astype(F32), ((0, 7), (0, TOK - starts.shape[1])))
    aux = jnp.concatenate([decay, begins], axis=0)

    send, rows = call(
        k_first,
        [(state_g, F32), ((16, TOK), F32)],
        1, core, aux, k, v,
        hbm=(2, 3),
        vmem_mib=53.5,
        scratch=[buffer, buffer, pltpu.SemaphoreType.DMA((2,))],
    )
    s_other = lax.ppermute(send, "seq", swap)
    s_mine, within = call(
        k_local,
        [(state_g, F32), (half, F32)],
        1, core, rows, q, k, v,
        hbm=(2, 3, 4),
        vmem_mib=53,
        scratch=[buffer, buffer, buffer, pltpu.SemaphoreType.DMA((3,))],
    )
    (pieces,) = call(k_pack, [((544, HEAD_DIM), F32)], 1, core, s_mine, s_other)
    pieces = trade(pieces.reshape(32, 1, 17 * HEAD_DIM)).reshape(544, HEAD_DIM)
    (entering,) = call(k_scan, [((32, 16, HEAD_DIM), F32)], 0, pieces)
    entering = trade(entering).reshape(state)
    e_mine, e_send = call(k_enter, [(state, F32)] * 2, 1, core, entering, s_mine, s_other)
    e_other = lax.ppermute(e_send, "seq", swap)
    att_mine, dnormed, within_other, part, inward = call(
        k_attend,
        [(half, F32), (wide, F32), (half, F32), ((2, TOK, HEAD_DIM), F32), (wide, F32)],
        1, core, rows, q, k, v, within, e_mine, gate, gain, up,
    )
    att_other, sums = call(
        k_sums,
        [(half, F32), ((8, TOK), F32)],
        1, core, q, within_other, inward, e_other, part, dnormed,
    )
    others = [around(sums, step) for step in (2, 1, 3)]
    weights, turned, mixings, factor, scaled = call(
        k_mid,
        [(square, F32), (square, F32), (square, BF16), (wide, F32), ((8, HEAD_DIM, TOK), BF16)],
        1, core, rows, q, k, gate, att_mine, att_other, dnormed, inward,
        cost_estimate=pl.CostEstimate(flops=4_000_000_000, bytes_accessed=8_000_000, transcendentals=1_000_000),
    )
    grad_other, b_send, inverses, projections = call(
        functools.partial(k_grad, features=float(features)),
        [(half, BF16), (state, F32), ((TOK, HEAD_DIM), F32), ((TOK, HEAD_DIM), F32)],
        0, sums, *others, att_other, dnormed, scaled,
    )
    b_other = lax.ppermute(b_send, "seq", swap)
    b_mine, grad_mine, gq, grad_gate, mixed_back = call(
        k_back,
        [(state, F32), (half, BF16), (wide, BF16), (wide, BF16), (square, BF16)],
        1, core, inverses, projections, att_mine, dnormed, grad_other, k, v,
        weights, turned, factor, inward, scaled, e_mine, e_other,
    )
    (back,) = call(k_pack_back, [((32, 16, HEAD_DIM), F32)], 1, core, b_mine, b_other, s_mine, s_other)
    back = trade(back)
    (leaving,) = call(k_scan_back, [((32, 16, HEAD_DIM), F32)], 0, back, pieces)
    leaving = trade(leaving).reshape(state)
    l_mine, l_send = call(k_leave, [(state, F32)] * 2, 1, core, leaving, b_mine, b_other, s_mine, s_other)
    l_other = lax.ppermute(l_send, "seq", swap)
    part_k, part_v, outward, k_mine, v_mine, grad_query, grad_gate = call(
        k_end_mine,
        [(half, F32), (half, F32), (half, F32), (half, BF16), (half, BF16), (wide, BF16), (wide, BF16)],
        1, core, rows, q, k, v, grad_mine, grad_other, mixed_back, mixings, l_mine, gq, grad_gate,
        hbm_out=(5, 6),
        scratch=[pltpu.SemaphoreType.DMA((2,))],
    )
    grad_key, grad_value = call(
        k_end,
        [(wide, BF16), (wide, BF16)],
        1, core, outward, k, v, part_k, part_v, l_other, k_mine, v_mine,
        hbm_out=(0, 1),
        scratch=[buffer, buffer, pltpu.SemaphoreType.DMA((10,))],
    )
    return grad_query, grad_key, grad_value, grad_gate


def solution(mesh):
    token = P("seq", "head")
    return jax.shard_map(
        local,
        mesh=mesh,
        in_specs=(token, token, token, P("head", "seq"), P("seq", None), token, P("head"), token),
        out_specs=(token,) * 4,
        check_vma=False,
    )
```

```python
import functools

import jax
import jax.numpy as jnp
from jax import lax
from jax.experimental import pallas as pl
from jax.experimental.pallas import tpu as pltpu
from jax.sharding import PartitionSpec as P

HEAD_DIM = 128
TOK = 256
HALF = 4
EPSILON = 1e-06
F32 = jnp.float32
BF16 = jnp.bfloat16
NEG = -1e30


def dot(a, b, ca, cb):
    return lax.dot_general(a, b, (((ca,), (cb,)), ((), ())), preferred_element_type=F32)


def parts(a, count):
    out = []
    for _ in range(count):
        out.append(a.astype(BF16))
        a = a - out[-1].astype(F32)
    return out


def wide_dot(a, state, axis):
    return dot(jnp.concatenate([a, a], axis=1), jnp.concatenate(parts(state, 2), axis=axis), 1, axis)


def call(kernel, outs, n_smem, *args, hbm=(), hbm_out=(), scratch=(), **kw):
    smem = pl.BlockSpec(memory_space=pltpu.SMEM)
    vmem = pl.BlockSpec(memory_space=pltpu.VMEM)
    far = pl.BlockSpec(memory_space=pltpu.HBM)
    args = [pltpu.with_memory_space_constraint(a, pltpu.HBM) if n in hbm else a for n, a in enumerate(args)]
    return pl.pallas_call(
        kernel,
        out_shape=[jax.ShapeDtypeStruct(s, d) for s, d in outs],
        in_specs=[smem] * n_smem + [far if n in hbm else vmem for n in range(n_smem, len(args))],
        out_specs=[far if n in hbm_out else vmem for n in range(len(outs))],
        scratch_shapes=list(scratch),
        compiler_params=pltpu.CompilerParams(vmem_limit_bytes=24 * 1024 * 1024),
        **kw,
    )(*args)


def cols(core, slot):
    return pl.ds(pl.multiple_of(((slot + HALF * core) % 8) * HEAD_DIM, HEAD_DIM), HEAD_DIM)


def half_cols(half):
    width = HALF * HEAD_DIM
    return pl.ds(pl.multiple_of(half * width, width), width)


def here(slot):
    return slice(slot * HEAD_DIM, (slot + 1) * HEAD_DIM)


def spread(lines, count):
    n = lines.shape[0]
    shape = (count * n, n * HEAD_DIM)
    line = lax.broadcasted_iota(jnp.int32, shape, 0) % n
    head = lax.broadcasted_iota(jnp.int32, shape, 1) // HEAD_DIM
    pick = (line == head).astype(F32).astype(BF16)
    return dot(jnp.concatenate(parts(lines, count), axis=0), pick, 0, 0)


def latest_of(rows):
    return rows[8:9, :]


def outward_of(rows, slots):
    row, latest = rows[slots, :], latest_of(rows)
    place = lax.broadcasted_iota(jnp.int32, row.shape, 1).astype(F32)
    kept = place >= latest[:, TOK - 1 : TOK]
    return jnp.exp(jnp.where(kept, row[:, TOK - 1 : TOK] - row, NEG))


def inward_of(rows):
    return jnp.exp(jnp.where(latest_of(rows) < 0, rows[0:8, :], NEG))


def through_of(rows):
    last = jnp.where(latest_of(rows)[:, TOK - 1 : TOK] < 0, rows[0:8, TOK - 1 : TOK], NEG)
    return jnp.broadcast_to(jnp.exp(last), (8, HEAD_DIM))


def state_of(left, scale, right):
    return dot((left.astype(F32) * scale).astype(BF16), right, 0, 0)


def fetch(pairs, sems):
    copies = [pltpu.make_async_copy(src, dst, sems.at[n]) for n, (src, dst) in enumerate(pairs)]
    for copy in copies:
        copy.start()
    return copies


def k_first(
    core_ref, starts_in, decay, q, k, v, send, rows, q_mine, k_mine, v_mine, kbuf, vbuf, dbuf, starts, sems
):
    core = core_ref[0]
    there = half_cols(1 - core)
    mine = half_cols(core)
    copies = fetch(
        [
            (decay, dbuf), (starts_in, starts), (k.at[:, there], kbuf), (v.at[:, there], vbuf),
            (k.at[:, mine], k_mine), (v.at[:, mine], v_mine), (q.at[:, mine], q_mine),
        ],
        sems,
    )
    a = lax.broadcasted_iota(jnp.int32, (TOK, TOK), 0)
    b = lax.broadcasted_iota(jnp.int32, (TOK, TOK), 1)
    copies[0].wait()
    d = dbuf[...]
    d = jnp.where(core == 0, d, jnp.concatenate([d[HALF:], d[:HALF]], axis=0))
    sums = dot(jnp.concatenate(parts(d, 3), axis=0), (a <= b).astype(BF16), 1, 0)
    rows[0:8, :] = sums[0:8] + sums[8:16] + sums[16:24]
    copies[1].wait()
    place = lax.broadcasted_iota(jnp.int32, (8, TOK), 1)
    latest = jnp.full((8, TOK), -1, jnp.int32)
    for j in range(4):
        begin = starts[0, j]
        latest = jnp.maximum(latest, jnp.where(begin <= place, begin, -1))
    rows[8:16, :] = latest.astype(F32)
    outward = spread(outward_of(rows, slice(HALF, 8)), 2)
    through = through_of(rows)
    send[512:520, :] = jnp.concatenate([through[HALF:8], through[0:HALF]], axis=0)
    copies[2].wait()
    copies[3].wait()
    for i in range(HALF):
        send[i * 128 : (i + 1) * 128, :] = state_of(kbuf[:, here(i)], outward[:, here(i)], vbuf[:, here(i)])
    for copy in copies[4:]:
        copy.wait()


def mixed(weight, query, key, value):
    return dot((weight * dot(query, key, 1, 1)).astype(BF16), value, 1, 0)


def biases(rows):
    latest = spread(latest_of(rows), 1)
    t = lax.broadcasted_iota(jnp.int32, (TOK, HEAD_DIM), 0)
    s = lax.broadcasted_iota(jnp.int32, (TOK, HEAD_DIM), 1)
    out = []
    for part in range(2):
        place = s + part * HEAD_DIM
        out.append(jnp.where(jnp.logical_and(place <= t, place.astype(F32) >= latest), 0.0, NEG))
    return out


def weight_of(rows, column, bias, slot):
    line = rows[slot : slot + 1, :]
    return jnp.concatenate(
        [jnp.exp(column - line[:, here(part)] + bias[part]) for part in range(2)], axis=1
    )


def k_local(rows, q, k, v, mine, within):
    columns = spread(rows[0:HALF, :], 3)
    bias = biases(rows)
    outward = spread(outward_of(rows, slice(0, HALF)), 2)
    mine[512:520, :] = through_of(rows)
    for i in range(HALF):
        mine[i * 128 : (i + 1) * 128, :] = state_of(k[:, here(i)], outward[:, here(i)], v[:, here(i)])
    for i in range(HALF):
        weight = weight_of(rows, columns[:, here(i)], bias, i)
        within[:, here(i)] = mixed(weight, q[:, here(i)], k[:, here(i)], v[:, here(i)])


def k_pack(core_ref, mine, other, out):
    first = core_ref[0] == 0
    for i in range(HALF):
        at = slice(i * 128, (i + 1) * 128)
        g_mine, g_other = mine[512 + i : 513 + i, :], other[512 + i : 513 + i, :]
        s_mine, s_other = mine[at, :], other[at, :]
        state = jnp.where(first, s_mine * g_other + s_other, s_other * g_mine + s_mine)
        for j in range(8):
            base = 17 * (8 * i + j)
            out[base : base + 16, :] = state[16 * j : 16 * (j + 1), :]
            out[base + 16 : base + 17, :] = g_mine * g_other


def k_scan(pieces, out):
    state = jnp.zeros((16, HEAD_DIM), F32)
    for i in range(32):
        out[i] = state
        state = state * pieces[17 * i + 16 : 17 * i + 17, :] + pieces[17 * i : 17 * i + 16, :]


def k_scan_back(pieces, factors, out):
    state = jnp.zeros((16, HEAD_DIM), F32)
    for i in reversed(range(32)):
        out[i] = state
        state = state * factors[17 * i + 16 : 17 * i + 17, :] + pieces[i]


def k_enter(core_ref, entering, mine, other, e_mine, e_send):
    first = core_ref[0] == 0
    for i in range(HALF):
        at = slice(i * 128, (i + 1) * 128)
        g0 = jnp.where(first, mine[512 + i : 513 + i, :], other[512 + i : 513 + i, :])
        s0 = jnp.where(first, mine[at, :], other[at, :])
        e0 = entering[at, :]
        e1 = e0 * g0 + s0
        e_mine[at, :] = jnp.where(first, e0, e1)
        e_send[at, :] = jnp.where(first, e1, e0)


def k_attend(
    core_ref, rows, q, k, v, within, e_mine, gate, gain, up,
    att_mine, dnormed, within_other, part, inward,
):
    core = core_ref[0]
    inward[...] = spread(inward_of(rows), 2)
    columns = spread(rows[HALF:8, :], 3)
    bias = biases(rows)
    squares = jnp.zeros((TOK, HEAD_DIM), F32)
    products = jnp.zeros((TOK, HEAD_DIM), F32)
    for slot in range(8):
        at = cols(core, slot)
        dn = up[:, at].astype(F32) * gain[:, at] * jax.nn.sigmoid(gate[:, at].astype(F32))
        dnormed[:, here(slot)] = dn
        if slot < HALF:
            carried = wide_dot(q[:, at], e_mine[slot * 128 : (slot + 1) * 128, :], 0)
            att = within[:, here(slot)] + carried * inward[:, here(slot)]
            att_mine[:, here(slot)] = att
            squares += att * att
            products += dn * att
        else:
            weight = weight_of(rows, columns[:, here(slot - HALF)], bias, slot)
            within_other[:, here(slot - HALF)] = mixed(weight, q[:, at], k[:, at], v[:, at])
    part[0] = squares
    part[1] = products


def k_sums(core_ref, q, within, inward, e_other, part, dnormed, att_other, sums):
    core = core_ref[0]
    squares, products = part[0], part[1]
    for i in range(HALF):
        slot = HALF + i
        carried = wide_dot(q[:, cols(core, slot)], e_other[i * 128 : (i + 1) * 128, :], 0)
        att = within[:, here(i)] + carried * inward[:, here(slot)]
        att_other[:, here(i)] = att
        squares += att * att
        products += dnormed[:, here(slot)] * att
    ones = jnp.ones((8, 2 * HEAD_DIM), BF16)
    line = lax.broadcasted_iota(jnp.int32, (8, TOK), 0)
    sums[...] = jnp.where(
        line < 4,
        dot(ones, jnp.concatenate(parts(squares, 2), axis=1), 1, 1),
        dot(ones, jnp.concatenate(parts(products, 2), axis=1), 1, 1),
    )


def k_mid(
    core_ref, rows, q, k, gate, att_mine, att_other, dnormed, inward,
    weights, turned, mixings, factor, scaled,
):
    core = core_ref[0]
    latest = latest_of(rows)
    columns = spread(rows[0:8, :], 3)
    biased = biases(rows)
    for slot in range(8):
        weights[slot] = weight_of(rows, columns[:, here(slot)], biased, slot)
    s = lax.broadcasted_iota(jnp.int32, (TOK, HEAD_DIM), 0)
    t = lax.broadcasted_iota(jnp.int32, (TOK, HEAD_DIM), 1)
    for part in range(2):
        at = here(part)
        kept = jnp.logical_and(s <= t + part * HEAD_DIM, s.astype(F32) >= latest[:, at])
        bias = jnp.where(kept, 0.0, NEG)
        for slot in range(8):
            turned[slot, :, at] = jnp.exp(rows[slot : slot + 1, at] - columns[:, here(slot)] + bias)
    for slot in reversed(range(8)):
        at = cols(core, slot)
        i = slot % HALF
        query = q[:, at]
        scaled[slot] = (query.astype(F32) * inward[:, here(slot)]).astype(BF16).T
        mixings[slot] = (turned[slot] * dot(k[:, at], query, 1, 1)).astype(BF16)
        att = (att_mine if slot < HALF else att_other)[:, here(i)]
        opening = jax.nn.sigmoid(gate[:, at].astype(F32))
        factor[:, here(slot)] = dnormed[:, here(slot)] * att * (1.0 - opening)


def grad_of(att, dnormed, inverse, projection):
    return ((dnormed - att * inverse * projection) * inverse).astype(BF16)


def k_grad(sums0, sums1, sums2, sums3, att, dnormed, scaled, grad, send, inverses, projections, *, features):
    total = sums0[...] + sums1[...] + sums2[...] + sums3[...]
    inverse = 1.0 / jnp.sqrt(total[0:1] / features + EPSILON)
    both = spread(jnp.concatenate([inverse, total[4:5] * inverse / features], axis=0), 3)
    inverse, projection = both[:, :HEAD_DIM], both[:, HEAD_DIM:]
    for i in range(HALF):
        slot = HALF + i
        value = grad_of(att[:, here(i)], dnormed[:, here(slot)], inverse, projection)
        grad[:, here(i)] = value
        send[i * 128 : (i + 1) * 128, :] = dot(scaled[slot], value, 1, 0)
    inverses[...] = inverse
    projections[...] = projection


def k_back(
    core_ref, inverses, projections, att_mine, dnormed, grad_other, k, v,
    weights, turned, factor, inward, scaled, e_mine, e_other,
    mine, grad_mine, gq, gate_out, mixed_back,
):
    core = core_ref[0]
    inverse, projection = inverses[...], projections[...]
    for slot in range(8):
        at = cols(core, slot)
        i = slot % HALF
        key, value = k[:, at], v[:, at]
        if slot < HALF:
            upstream = grad_of(att_mine[:, here(i)], dnormed[:, here(slot)], inverse, projection)
            grad_mine[:, here(i)] = upstream
            mine[i * 128 : (i + 1) * 128, :] = dot(scaled[slot], upstream, 1, 0)
        else:
            upstream = grad_other[:, here(i)]
        grad_mixing = (weights[slot] * dot(upstream, value, 1, 1)).astype(BF16)
        mixed_back[slot] = (turned[slot] * dot(value, upstream, 1, 1)).astype(BF16)
        state = (e_mine if slot < HALF else e_other)[i * 128 : (i + 1) * 128, :]
        carried = wide_dot(upstream, state, 1)
        gq[:, at] = (dot(grad_mixing, key, 1, 0) + carried * inward[:, here(slot)]).astype(BF16)
        gate_out[:, at] = (factor[:, here(slot)] * inverse).astype(BF16)


def k_pack_back(core_ref, mine, other, s_mine, s_other, out):
    first = core_ref[0] == 0
    for i in range(HALF):
        at = slice(i * 128, (i + 1) * 128)
        g0 = jnp.where(first, s_mine[512 + i : 513 + i, :], s_other[512 + i : 513 + i, :])
        b_mine, b_other = mine[at, :], other[at, :]
        state = jnp.where(first, b_mine + g0 * b_other, b_other + g0 * b_mine)
        for j in range(8):
            out[8 * i + j] = state[16 * j : 16 * (j + 1), :]


def k_leave(core_ref, leaving, mine, other, s_mine, s_other, l_mine, l_send):
    first = core_ref[0] == 0
    for i in range(HALF):
        at = slice(i * 128, (i + 1) * 128)
        g1 = jnp.where(first, s_other[512 + i : 513 + i, :], s_mine[512 + i : 513 + i, :])
        b1 = jnp.where(first, other[at, :], mine[at, :])
        l1 = leaving[at, :]
        l0 = l1 * g1 + b1
        l_mine[at, :] = jnp.where(first, l0, l1)
        l_send[at, :] = jnp.where(first, l1, l0)


def finish(state, scale, key, value, part_k, part_v):
    to_key = wide_dot(value, state, 1)
    to_value = wide_dot(key, state, 0)
    return (part_k + to_key * scale).astype(BF16), (part_v + to_value * scale).astype(BF16)


def k_end_mine(
    core_ref, rows, q, k, v, grad_mine, grad_other, mixed_back, mixings, l_mine, gq, gate_in,
    part_k, part_v, outward_other, k_mine, v_mine, out_q, out_gate, sems,
):
    core = core_ref[0]
    copies = fetch([(gq, out_q), (gate_in, out_gate)], sems)
    outward = spread(outward_of(rows, slice(0, 8)), 2)
    outward_other[...] = outward[:, 512:]
    for slot in range(8):
        i = slot % HALF
        at = cols(core, slot)
        upstream = (grad_mine if slot < HALF else grad_other)[:, here(i)]
        to_key = dot(mixed_back[slot], q[:, at], 1, 0)
        to_value = dot(mixings[slot], upstream, 1, 0)
        if slot < HALF:
            state = l_mine[i * 128 : (i + 1) * 128, :]
            k_mine[:, here(i)], v_mine[:, here(i)] = finish(
                state, outward[:, here(slot)], k[:, at], v[:, at], to_key, to_value
            )
        else:
            part_k[:, here(i)] = to_key
            part_v[:, here(i)] = to_value
    for copy in copies:
        copy.wait()


def k_end(
    core_ref, outward, k, v, part_k, part_v, l_other, k_mine, v_mine,
    out_k, out_v, kbuf, vbuf, sems,
):
    core = core_ref[0]
    there = half_cols(core)
    copies = fetch([(k_mine, out_k.at[:, there]), (v_mine, out_v.at[:, there])], sems)
    for i in range(HALF):
        slot = HALF + i
        at = cols(core, slot)
        state = l_other[i * 128 : (i + 1) * 128, :]
        kbuf[:, here(i)], vbuf[:, here(i)] = finish(
            state, outward[:, here(i)], k[:, at], v[:, at], part_k[:, here(i)], part_v[:, here(i)]
        )
        for n, (buf, out) in enumerate(((kbuf, out_k), (vbuf, out_v))):
            copies.append(pltpu.make_async_copy(buf.at[:, here(i)], out.at[:, at], sems.at[2 + 2 * i + n]))
            copies[-1].start()
    for copy in copies:
        copy.wait()


def local(q, k, v, decay, starts, gate, gain, up):
    places = lax.axis_size("seq")
    swap = [(i, i ^ 1) for i in range(places)]
    groups = [list(range(c, places, 2)) for c in range(2)]
    core = (lax.axis_index("seq") % 2).astype(jnp.int32).reshape(1)
    heads = lax.axis_size("head")
    features = q.shape[1] * heads
    gain = gain.reshape(1, -1)
    wide, half = (TOK, 1024), (TOK, 512)
    state, state_g = (512, HEAD_DIM), (520, HEAD_DIM)
    square = (8, TOK, TOK)
    buffer = pltpu.VMEM(half, BF16)

    def trade(a):
        return lax.all_to_all(a, "seq", 0, 0, axis_index_groups=groups)

    def around(a, step):
        return lax.ppermute(a, "head", [(i, (i + step) % heads) for i in range(heads)])

    send, rows, *own = call(
        k_first,
        [(state_g, F32), ((16, TOK), F32)] + [(half, BF16)] * 3,
        1, core, starts, decay, q, k, v,
        hbm=(1, 2, 3, 4, 5),
        scratch=[
            buffer, buffer, pltpu.VMEM((8, TOK), F32), pltpu.SMEM((1, 4), jnp.int32), pltpu.SemaphoreType.DMA((7,)),
        ],
    )
    s_other = lax.ppermute(send, "seq", swap)
    s_mine, within = call(
        k_local,
        [(state_g, F32), (half, F32)],
        0, rows, *own,
    )
    (pieces,) = call(k_pack, [((544, HEAD_DIM), F32)], 1, core, s_mine, s_other)
    pieces = trade(pieces.reshape(32, 1, 17 * HEAD_DIM)).reshape(544, HEAD_DIM)
    (entering,) = call(k_scan, [((32, 16, HEAD_DIM), F32)], 0, pieces)
    entering = trade(entering).reshape(state)
    e_mine, e_send = call(k_enter, [(state, F32)] * 2, 1, core, entering, s_mine, s_other)
    e_other = lax.ppermute(e_send, "seq", swap)
    att_mine, dnormed, within_other, part, inward = call(
        k_attend,
        [(half, F32), (wide, F32), (half, F32), ((2, TOK, HEAD_DIM), F32), (wide, F32)],
        1, core, rows, q, k, v, within, e_mine, gate, gain, up,
    )
    att_other, sums = call(
        k_sums,
        [(half, F32), ((8, TOK), F32)],
        1, core, q, within_other, inward, e_other, part, dnormed,
    )
    others = [around(sums, step) for step in (2, 1, 3)]
    weights, turned, mixings, factor, scaled = call(
        k_mid,
        [(square, F32), (square, F32), (square, BF16), (wide, F32), ((8, HEAD_DIM, TOK), BF16)],
        1, core, rows, q, k, gate, att_mine, att_other, dnormed, inward,
        cost_estimate=pl.CostEstimate(flops=4_000_000_000, bytes_accessed=8_000_000, transcendentals=1_000_000),
    )
    grad_other, b_send, inverses, projections = call(
        functools.partial(k_grad, features=float(features)),
        [(half, BF16), (state, F32), ((TOK, HEAD_DIM), F32), ((TOK, HEAD_DIM), F32)],
        0, sums, *others, att_other, dnormed, scaled,
    )
    b_other = lax.ppermute(b_send, "seq", swap)
    b_mine, grad_mine, gq, grad_gate, mixed_back = call(
        k_back,
        [(state, F32), (half, BF16), (wide, BF16), (wide, BF16), (square, BF16)],
        1, core, inverses, projections, att_mine, dnormed, grad_other, k, v,
        weights, turned, factor, inward, scaled, e_mine, e_other,
    )
    (back,) = call(k_pack_back, [((32, 16, HEAD_DIM), F32)], 1, core, b_mine, b_other, s_mine, s_other)
    back = trade(back)
    (leaving,) = call(k_scan_back, [((32, 16, HEAD_DIM), F32)], 0, back, pieces)
    leaving = trade(leaving).reshape(state)
    l_mine, l_send = call(k_leave, [(state, F32)] * 2, 1, core, leaving, b_mine, b_other, s_mine, s_other)
    l_other = lax.ppermute(l_send, "seq", swap)
    part_k, part_v, outward, k_mine, v_mine, grad_query, grad_gate = call(
        k_end_mine,
        [(half, F32), (half, F32), (half, F32), (half, BF16), (half, BF16), (wide, BF16), (wide, BF16)],
        1, core, rows, q, k, v, grad_mine, grad_other, mixed_back, mixings, l_mine, gq, grad_gate,
        hbm_out=(5, 6),
        scratch=[pltpu.SemaphoreType.DMA((2,))],
    )
    grad_key, grad_value = call(
        k_end,
        [(wide, BF16), (wide, BF16)],
        1, core, outward, k, v, part_k, part_v, l_other, k_mine, v_mine,
        hbm_out=(0, 1),
        scratch=[buffer, buffer, pltpu.SemaphoreType.DMA((10,))],
    )
    return grad_query, grad_key, grad_value, grad_gate


def solution(mesh):
    token = P("seq", "head")
    return jax.shard_map(
        local,
        mesh=mesh,
        in_specs=(token, token, token, P("head", "seq"), P("seq", None), token, P("head"), token),
        out_specs=(token,) * 4,
        check_vma=False,
    )
```

```python
import functools

import jax
import jax.numpy as jnp
from jax import lax
from jax.experimental import pallas as pl
from jax.experimental.pallas import tpu as pltpu
from jax.sharding import PartitionSpec as P

HEAD_DIM = 128
TOK = 256
HALF = 4
EPSILON = 1e-06
F32 = jnp.float32
BF16 = jnp.bfloat16
NEG = -1e30


def dot(a, b, ca, cb):
    return lax.dot_general(a, b, (((ca,), (cb,)), ((), ())), preferred_element_type=F32)


def parts(a, count):
    out = []
    for _ in range(count):
        out.append(a.astype(BF16))
        a = a - out[-1].astype(F32)
    return out


def wide_dot(a, state, axis):
    return dot(jnp.concatenate([a, a], axis=1), jnp.concatenate(parts(state, 2), axis=axis), 1, axis)


def call(kernel, outs, n_smem, *args, hbm=(), hbm_out=(), scratch=(), **kw):
    smem = pl.BlockSpec(memory_space=pltpu.SMEM)
    vmem = pl.BlockSpec(memory_space=pltpu.VMEM)
    far = pl.BlockSpec(memory_space=pltpu.HBM)
    args = [pltpu.with_memory_space_constraint(a, pltpu.HBM) if n in hbm else a for n, a in enumerate(args)]
    return pl.pallas_call(
        kernel,
        out_shape=[jax.ShapeDtypeStruct(s, d) for s, d in outs],
        in_specs=[smem] * n_smem + [far if n in hbm else vmem for n in range(n_smem, len(args))],
        out_specs=[far if n in hbm_out else vmem for n in range(len(outs))],
        scratch_shapes=list(scratch),
        compiler_params=pltpu.CompilerParams(vmem_limit_bytes=24 * 1024 * 1024),
        **kw,
    )(*args)


def cols(core, slot):
    return pl.ds(pl.multiple_of(((slot + HALF * core) % 8) * HEAD_DIM, HEAD_DIM), HEAD_DIM)


def half_cols(half):
    width = HALF * HEAD_DIM
    return pl.ds(pl.multiple_of(half * width, width), width)


def here(slot):
    return slice(slot * HEAD_DIM, (slot + 1) * HEAD_DIM)


def spread(lines, count):
    n = lines.shape[0]
    shape = (count * n, n * HEAD_DIM)
    line = lax.broadcasted_iota(jnp.int32, shape, 0) % n
    head = lax.broadcasted_iota(jnp.int32, shape, 1) // HEAD_DIM
    pick = (line == head).astype(F32).astype(BF16)
    return dot(jnp.concatenate(parts(lines, count), axis=0), pick, 0, 0)


def latest_of(rows):
    return rows[8:9, :]


def outward_of(rows, slots):
    row, latest = rows[slots, :], latest_of(rows)
    place = lax.broadcasted_iota(jnp.int32, row.shape, 1).astype(F32)
    kept = place >= latest[:, TOK - 1 : TOK]
    return jnp.exp(jnp.where(kept, row[:, TOK - 1 : TOK] - row, NEG))


def inward_of(rows):
    return jnp.exp(jnp.where(latest_of(rows) < 0, rows[0:8, :], NEG))


def through_of(rows):
    last = jnp.where(latest_of(rows)[:, TOK - 1 : TOK] < 0, rows[0:8, TOK - 1 : TOK], NEG)
    return jnp.broadcast_to(jnp.exp(last), (8, HEAD_DIM))


def turn(left, line):
    return (left.T.astype(F32) * line).astype(BF16)


def fetch(pairs, sems):
    copies = [pltpu.make_async_copy(src, dst, sems.at[n]) for n, (src, dst) in enumerate(pairs)]
    for copy in copies:
        copy.start()
    return copies


def k_first(
    core_ref, starts_in, decay, q, k, v, send, rows, q_mine, k_mine, v_mine, kbuf, vbuf, dbuf, starts, sems
):
    core = core_ref[0]
    there = half_cols(1 - core)
    mine = half_cols(core)
    copies = fetch(
        [
            (decay, dbuf), (starts_in, starts), (k.at[:, there], kbuf), (v.at[:, there], vbuf),
            (k.at[:, mine], k_mine), (v.at[:, mine], v_mine), (q.at[:, mine], q_mine),
        ],
        sems,
    )
    a = lax.broadcasted_iota(jnp.int32, (TOK, TOK), 0)
    b = lax.broadcasted_iota(jnp.int32, (TOK, TOK), 1)
    copies[0].wait()
    d = dbuf[...]
    d = jnp.where(core == 0, d, jnp.concatenate([d[HALF:], d[:HALF]], axis=0))
    sums = dot(jnp.concatenate(parts(d, 3), axis=0), (a <= b).astype(BF16), 1, 0)
    rows[0:8, :] = sums[0:8] + sums[8:16] + sums[16:24]
    copies[1].wait()
    place = lax.broadcasted_iota(jnp.int32, (8, TOK), 1)
    latest = jnp.full((8, TOK), -1, jnp.int32)
    for j in range(4):
        begin = starts[0, j]
        latest = jnp.maximum(latest, jnp.where(begin <= place, begin, -1))
    rows[8:16, :] = latest.astype(F32)
    outward = outward_of(rows, slice(HALF, 8))
    through = through_of(rows)
    send[512:520, :] = jnp.concatenate([through[HALF:8], through[0:HALF]], axis=0)
    copies[2].wait()
    copies[3].wait()
    for i in range(HALF):
        turned = turn(kbuf[:, here(i)], outward[i : i + 1, :])
        send[i * 128 : (i + 1) * 128, :] = dot(turned, vbuf[:, here(i)], 1, 0)
    for copy in copies[4:]:
        copy.wait()


def mixed(weight, query, key, value):
    return dot((weight * dot(query, key, 1, 1)).astype(BF16), value, 1, 0)


def biases(rows):
    latest = spread(latest_of(rows), 1)
    t = lax.broadcasted_iota(jnp.int32, (TOK, HEAD_DIM), 0)
    s = lax.broadcasted_iota(jnp.int32, (TOK, HEAD_DIM), 1)
    out = []
    for part in range(2):
        place = s + part * HEAD_DIM
        out.append(jnp.where(jnp.logical_and(place <= t, place.astype(F32) >= latest), 0.0, NEG))
    return out


def weight_of(rows, column, bias, slot):
    line = rows[slot : slot + 1, :]
    return jnp.concatenate(
        [jnp.exp(column - line[:, here(part)] + bias[part]) for part in range(2)], axis=1
    )


def k_local(rows, q, k, v, mine, within, summed, inward):
    inward[...] = spread(inward_of(rows), 2)
    columns = spread(rows[0:8, :], 3)
    summed[...] = columns
    bias = biases(rows)
    outward = outward_of(rows, slice(0, HALF))
    mine[512:520, :] = through_of(rows)
    for i in range(HALF):
        turned = turn(k[:, here(i)], outward[i : i + 1, :])
        mine[i * 128 : (i + 1) * 128, :] = dot(turned, v[:, here(i)], 1, 0)
    for i in range(HALF):
        weight = weight_of(rows, columns[:, here(i)], bias, i)
        within[:, here(i)] = mixed(weight, q[:, here(i)], k[:, here(i)], v[:, here(i)])


def k_pack(core_ref, mine, other, out):
    first = core_ref[0] == 0
    for i in range(HALF):
        at = slice(i * 128, (i + 1) * 128)
        g_mine, g_other = mine[512 + i : 513 + i, :], other[512 + i : 513 + i, :]
        s_mine, s_other = mine[at, :], other[at, :]
        state = jnp.where(first, s_mine * g_other + s_other, s_other * g_mine + s_mine)
        for j in range(8):
            base = 17 * (8 * i + j)
            out[base : base + 16, :] = state[16 * j : 16 * (j + 1), :]
            out[base + 16 : base + 17, :] = g_mine * g_other


def k_scan(pieces, out):
    state = jnp.zeros((16, HEAD_DIM), F32)
    for i in range(32):
        out[i] = state
        state = state * pieces[17 * i + 16 : 17 * i + 17, :] + pieces[17 * i : 17 * i + 16, :]


def k_scan_back(pieces, factors, out):
    state = jnp.zeros((16, HEAD_DIM), F32)
    for i in reversed(range(32)):
        out[i] = state
        state = state * factors[17 * i + 16 : 17 * i + 17, :] + pieces[i]


def k_enter(core_ref, entering, mine, other, e_mine, e_send):
    first = core_ref[0] == 0
    for i in range(HALF):
        at = slice(i * 128, (i + 1) * 128)
        g0 = jnp.where(first, mine[512 + i : 513 + i, :], other[512 + i : 513 + i, :])
        s0 = jnp.where(first, mine[at, :], other[at, :])
        e0 = entering[at, :]
        e1 = e0 * g0 + s0
        e_mine[at, :] = jnp.where(first, e0, e1)
        e_send[at, :] = jnp.where(first, e1, e0)


def k_attend(
    core_ref, rows, summed, q, k, v, within, inward, e_mine, gate, gain, up,
    att_mine, dnormed, within_other, part,
):
    core = core_ref[0]
    bias = biases(rows)
    squares = jnp.zeros((TOK, HEAD_DIM), F32)
    products = jnp.zeros((TOK, HEAD_DIM), F32)
    for slot in range(8):
        at = cols(core, slot)
        dn = up[:, at].astype(F32) * gain[:, at] * jax.nn.sigmoid(gate[:, at].astype(F32))
        dnormed[:, here(slot)] = dn
        if slot < HALF:
            carried = wide_dot(q[:, at], e_mine[slot * 128 : (slot + 1) * 128, :], 0)
            att = within[:, here(slot)] + carried * inward[:, here(slot)]
            att_mine[:, here(slot)] = att
            squares += att * att
            products += dn * att
        else:
            weight = weight_of(rows, summed[:, here(slot)], bias, slot)
            within_other[:, here(slot - HALF)] = mixed(weight, q[:, at], k[:, at], v[:, at])
    part[0] = squares
    part[1] = products


def k_sums(core_ref, q, within, inward, e_other, part, dnormed, att_other, sums):
    core = core_ref[0]
    squares, products = part[0], part[1]
    for i in range(HALF):
        slot = HALF + i
        carried = wide_dot(q[:, cols(core, slot)], e_other[i * 128 : (i + 1) * 128, :], 0)
        att = within[:, here(i)] + carried * inward[:, here(slot)]
        att_other[:, here(i)] = att
        squares += att * att
        products += dnormed[:, here(slot)] * att
    ones = jnp.ones((8, 2 * HEAD_DIM), BF16)
    line = lax.broadcasted_iota(jnp.int32, (8, TOK), 0)
    sums[...] = jnp.where(
        line < 4,
        dot(ones, jnp.concatenate(parts(squares, 2), axis=1), 1, 1),
        dot(ones, jnp.concatenate(parts(products, 2), axis=1), 1, 1),
    )


def k_mid(
    core_ref, rows, summed, q, k, gate, att_mine, att_other, dnormed,
    weights, turned, mixings, factor, scaled, outward,
):
    core = core_ref[0]
    latest = latest_of(rows)
    outward[...] = spread(outward_of(rows, slice(0, 8)), 2)
    biased = biases(rows)
    for slot in range(8):
        weights[slot] = weight_of(rows, summed[:, here(slot)], biased, slot)
    s = lax.broadcasted_iota(jnp.int32, (TOK, HEAD_DIM), 0)
    t = lax.broadcasted_iota(jnp.int32, (TOK, HEAD_DIM), 1)
    for part in range(2):
        at = here(part)
        kept = jnp.logical_and(s <= t + part * HEAD_DIM, s.astype(F32) >= latest[:, at])
        bias = jnp.where(kept, 0.0, NEG)
        for slot in range(8):
            turned[slot, :, at] = jnp.exp(rows[slot : slot + 1, at] - summed[:, here(slot)] + bias)
    lines = inward_of(rows)
    for slot in reversed(range(8)):
        at = cols(core, slot)
        i = slot % HALF
        query = q[:, at]
        scaled[slot] = turn(query, lines[slot : slot + 1, :])
        mixings[slot] = (turned[slot] * dot(k[:, at], query, 1, 1)).astype(BF16)
        att = (att_mine if slot < HALF else att_other)[:, here(i)]
        opening = jax.nn.sigmoid(gate[:, at].astype(F32))
        factor[:, here(slot)] = dnormed[:, here(slot)] * att * (1.0 - opening)


def grad_of(att, dnormed, inverse, projection):
    return ((dnormed - att * inverse * projection) * inverse).astype(BF16)


def k_grad(sums0, sums1, sums2, sums3, att, dnormed, scaled, grad, send, inverses, projections, *, features):
    total = sums0[...] + sums1[...] + sums2[...] + sums3[...]
    inverse = 1.0 / jnp.sqrt(total[0:1] / features + EPSILON)
    both = spread(jnp.concatenate([inverse, total[4:5] * inverse / features], axis=0), 3)
    inverse, projection = both[:, :HEAD_DIM], both[:, HEAD_DIM:]
    for i in range(HALF):
        slot = HALF + i
        value = grad_of(att[:, here(i)], dnormed[:, here(slot)], inverse, projection)
        grad[:, here(i)] = value
        send[i * 128 : (i + 1) * 128, :] = dot(scaled[slot], value, 1, 0)
    inverses[...] = inverse
    projections[...] = projection


def k_back(
    core_ref, inverses, projections, att_mine, dnormed, grad_other, k, v,
    weights, turned, factor, inward, scaled, e_mine, e_other,
    mine, grad_mine, gq, gate_out, mixed_back,
):
    core = core_ref[0]
    inverse, projection = inverses[...], projections[...]
    for slot in range(8):
        at = cols(core, slot)
        i = slot % HALF
        key, value = k[:, at], v[:, at]
        if slot < HALF:
            upstream = grad_of(att_mine[:, here(i)], dnormed[:, here(slot)], inverse, projection)
            grad_mine[:, here(i)] = upstream
            mine[i * 128 : (i + 1) * 128, :] = dot(scaled[slot], upstream, 1, 0)
        else:
            upstream = grad_other[:, here(i)]
        grad_mixing = (weights[slot] * dot(upstream, value, 1, 1)).astype(BF16)
        mixed_back[slot] = (turned[slot] * dot(value, upstream, 1, 1)).astype(BF16)
        state = (e_mine if slot < HALF else e_other)[i * 128 : (i + 1) * 128, :]
        carried = wide_dot(upstream, state, 1)
        gq[:, at] = (dot(grad_mixing, key, 1, 0) + carried * inward[:, here(slot)]).astype(BF16)
        gate_out[:, at] = (factor[:, here(slot)] * inverse).astype(BF16)


def k_pack_back(core_ref, mine, other, s_mine, s_other, out):
    first = core_ref[0] == 0
    for i in range(HALF):
        at = slice(i * 128, (i + 1) * 128)
        g0 = jnp.where(first, s_mine[512 + i : 513 + i, :], s_other[512 + i : 513 + i, :])
        b_mine, b_other = mine[at, :], other[at, :]
        state = jnp.where(first, b_mine + g0 * b_other, b_other + g0 * b_mine)
        for j in range(8):
            out[8 * i + j] = state[16 * j : 16 * (j + 1), :]


def k_leave(core_ref, leaving, mine, other, s_mine, s_other, l_mine, l_send):
    first = core_ref[0] == 0
    for i in range(HALF):
        at = slice(i * 128, (i + 1) * 128)
        g1 = jnp.where(first, s_other[512 + i : 513 + i, :], s_mine[512 + i : 513 + i, :])
        b1 = jnp.where(first, other[at, :], mine[at, :])
        l1 = leaving[at, :]
        l0 = l1 * g1 + b1
        l_mine[at, :] = jnp.where(first, l0, l1)
        l_send[at, :] = jnp.where(first, l1, l0)


def finish(state, scale, key, value, part_k, part_v):
    to_key = wide_dot(value, state, 1)
    to_value = wide_dot(key, state, 0)
    return (part_k + to_key * scale).astype(BF16), (part_v + to_value * scale).astype(BF16)


def upper_dot(mixed_to, slot, right):
    half = TOK // 2
    return jnp.concatenate(
        [
            dot(mixed_to[slot, :half, :], right, 1, 0),
            dot(mixed_to[slot, half:, half:], right[half:], 1, 0),
        ],
        axis=0,
    )


def k_end_mine(
    core_ref, outward, q, k, v, grad_mine, grad_other, mixed_back, mixings, l_mine, gq, gate_in,
    part_k, part_v, k_mine, v_mine, out_q, out_gate, sems,
):
    core = core_ref[0]
    copies = fetch([(gq, out_q), (gate_in, out_gate)], sems)
    for slot in range(8):
        i = slot % HALF
        at = cols(core, slot)
        upstream = (grad_mine if slot < HALF else grad_other)[:, here(i)]
        to_key = upper_dot(mixed_back, slot, q[:, at])
        to_value = upper_dot(mixings, slot, upstream)
        if slot < HALF:
            state = l_mine[i * 128 : (i + 1) * 128, :]
            k_mine[:, here(i)], v_mine[:, here(i)] = finish(
                state, outward[:, here(slot)], k[:, at], v[:, at], to_key, to_value
            )
        else:
            part_k[:, here(i)] = to_key
            part_v[:, here(i)] = to_value
    for copy in copies:
        copy.wait()


def k_end(
    core_ref, outward, k, v, part_k, part_v, l_other, k_mine, v_mine,
    out_k, out_v, kbuf, vbuf, sems,
):
    core = core_ref[0]
    there = half_cols(core)
    copies = fetch([(k_mine, out_k.at[:, there]), (v_mine, out_v.at[:, there])], sems)
    for i in range(HALF):
        slot = HALF + i
        at = cols(core, slot)
        state = l_other[i * 128 : (i + 1) * 128, :]
        kbuf[:, here(i)], vbuf[:, here(i)] = finish(
            state, outward[:, here(slot)], k[:, at], v[:, at], part_k[:, here(i)], part_v[:, here(i)]
        )
        for n, (buf, out) in enumerate(((kbuf, out_k), (vbuf, out_v))):
            copies.append(pltpu.make_async_copy(buf.at[:, here(i)], out.at[:, at], sems.at[2 + 2 * i + n]))
            copies[-1].start()
    for copy in copies:
        copy.wait()


def local(q, k, v, decay, starts, gate, gain, up):
    places = lax.axis_size("seq")
    swap = [(i, i ^ 1) for i in range(places)]
    groups = [list(range(c, places, 2)) for c in range(2)]
    core = (lax.axis_index("seq") % 2).astype(jnp.int32).reshape(1)
    heads = lax.axis_size("head")
    features = q.shape[1] * heads
    gain = gain.reshape(1, -1)
    wide, half = (TOK, 1024), (TOK, 512)
    state, state_g = (512, HEAD_DIM), (520, HEAD_DIM)
    square = (8, TOK, TOK)
    buffer = pltpu.VMEM(half, BF16)

    def trade(a):
        return lax.all_to_all(a, "seq", 0, 0, axis_index_groups=groups)

    def around(a, step):
        return lax.ppermute(a, "head", [(i, (i + step) % heads) for i in range(heads)])

    send, rows, *own = call(
        k_first,
        [(state_g, F32), ((16, TOK), F32)] + [(half, BF16)] * 3,
        1, core, starts, decay, q, k, v,
        hbm=(1, 2, 3, 4, 5),
        scratch=[
            buffer, buffer, pltpu.VMEM((8, TOK), F32), pltpu.SMEM((1, 4), jnp.int32), pltpu.SemaphoreType.DMA((7,)),
        ],
    )
    s_other = lax.ppermute(send, "seq", swap)
    s_mine, within, summed, inward = call(
        k_local,
        [(state_g, F32), (half, F32), (wide, F32), (wide, F32)],
        0, rows, *own,
    )
    (pieces,) = call(k_pack, [((544, HEAD_DIM), F32)], 1, core, s_mine, s_other)
    pieces = trade(pieces.reshape(32, 1, 17 * HEAD_DIM)).reshape(544, HEAD_DIM)
    (entering,) = call(k_scan, [((32, 16, HEAD_DIM), F32)], 0, pieces)
    entering = trade(entering).reshape(state)
    e_mine, e_send = call(k_enter, [(state, F32)] * 2, 1, core, entering, s_mine, s_other)
    e_other = lax.ppermute(e_send, "seq", swap)
    att_mine, dnormed, within_other, part = call(
        k_attend,
        [(half, F32), (wide, F32), (half, F32), ((2, TOK, HEAD_DIM), F32)],
        1, core, rows, summed, q, k, v, within, inward, e_mine, gate, gain, up,
    )
    att_other, sums = call(
        k_sums,
        [(half, F32), ((8, TOK), F32)],
        1, core, q, within_other, inward, e_other, part, dnormed,
    )
    others = [around(sums, step) for step in (2, 1, 3)]
    weights, turned, mixings, factor, scaled, outward = call(
        k_mid,
        [(square, F32), (square, F32), (square, BF16), (wide, F32), ((8, HEAD_DIM, TOK), BF16), (wide, F32)],
        1, core, rows, summed, q, k, gate, att_mine, att_other, dnormed,
        cost_estimate=pl.CostEstimate(flops=4_000_000_000, bytes_accessed=8_000_000, transcendentals=1_000_000),
    )
    grad_other, b_send, inverses, projections = call(
        functools.partial(k_grad, features=float(features)),
        [(half, BF16), (state, F32), ((TOK, HEAD_DIM), F32), ((TOK, HEAD_DIM), F32)],
        0, sums, *others, att_other, dnormed, scaled,
    )
    b_other = lax.ppermute(b_send, "seq", swap)
    b_mine, grad_mine, gq, grad_gate, mixed_back = call(
        k_back,
        [(state, F32), (half, BF16), (wide, BF16), (wide, BF16), (square, BF16)],
        1, core, inverses, projections, att_mine, dnormed, grad_other, k, v,
        weights, turned, factor, inward, scaled, e_mine, e_other,
    )
    (back,) = call(k_pack_back, [((32, 16, HEAD_DIM), F32)], 1, core, b_mine, b_other, s_mine, s_other)
    back = trade(back)
    (leaving,) = call(k_scan_back, [((32, 16, HEAD_DIM), F32)], 0, back, pieces)
    leaving = trade(leaving).reshape(state)
    l_mine, l_send = call(k_leave, [(state, F32)] * 2, 1, core, leaving, b_mine, b_other, s_mine, s_other)
    l_other = lax.ppermute(l_send, "seq", swap)
    part_k, part_v, k_mine, v_mine, grad_query, grad_gate = call(
        k_end_mine,
        [(half, F32), (half, F32), (half, BF16), (half, BF16), (wide, BF16), (wide, BF16)],
        1, core, outward, q, k, v, grad_mine, grad_other, mixed_back, mixings, l_mine, gq, grad_gate,
        hbm_out=(4, 5),
        scratch=[pltpu.SemaphoreType.DMA((2,))],
    )
    grad_key, grad_value = call(
        k_end,
        [(wide, BF16), (wide, BF16)],
        1, core, outward, k, v, part_k, part_v, l_other, k_mine, v_mine,
        hbm_out=(0, 1),
        scratch=[buffer, buffer, pltpu.SemaphoreType.DMA((10,))],
    )
    return grad_query, grad_key, grad_value, grad_gate


def solution(mesh):
    token = P("seq", "head")
    return jax.shard_map(
        local,
        mesh=mesh,
        in_specs=(token, token, token, P("head", "seq"), P("seq", None), token, P("head"), token),
        out_specs=(token,) * 4,
        check_vma=False,
    )
```

```python
import functools

import jax
import jax.numpy as jnp
from jax import lax
from jax.experimental import pallas as pl
from jax.experimental.pallas import tpu as pltpu
from jax.sharding import PartitionSpec as P

HEAD_DIM = 128
TOK = 256
HALF = 4
EPSILON = 1e-06
F32 = jnp.float32
BF16 = jnp.bfloat16
NEG = -1e30


def dot(a, b, ca, cb):
    return lax.dot_general(a, b, (((ca,), (cb,)), ((), ())), preferred_element_type=F32)


def parts(a, count):
    out = []
    for _ in range(count):
        out.append(a.astype(BF16))
        a = a - out[-1].astype(F32)
    return out


def wide_dot(a, state, axis):
    return dot(jnp.concatenate([a, a], axis=1), jnp.concatenate(parts(state, 2), axis=axis), 1, axis)


def call(kernel, outs, n_smem, *args, hbm=(), hbm_out=(), scratch=(), **kw):
    smem = pl.BlockSpec(memory_space=pltpu.SMEM)
    vmem = pl.BlockSpec(memory_space=pltpu.VMEM)
    far = pl.BlockSpec(memory_space=pltpu.HBM)
    args = [pltpu.with_memory_space_constraint(a, pltpu.HBM) if n in hbm else a for n, a in enumerate(args)]
    return pl.pallas_call(
        kernel,
        out_shape=[jax.ShapeDtypeStruct(s, d) for s, d in outs],
        in_specs=[smem] * n_smem + [far if n in hbm else vmem for n in range(n_smem, len(args))],
        out_specs=[far if n in hbm_out else vmem for n in range(len(outs))],
        scratch_shapes=list(scratch),
        compiler_params=pltpu.CompilerParams(vmem_limit_bytes=24 * 1024 * 1024),
        **kw,
    )(*args)


def cols(core, slot):
    return pl.ds(pl.multiple_of(((slot + HALF * core) % 8) * HEAD_DIM, HEAD_DIM), HEAD_DIM)


def half_cols(half):
    width = HALF * HEAD_DIM
    return pl.ds(pl.multiple_of(half * width, width), width)


def here(slot):
    return slice(slot * HEAD_DIM, (slot + 1) * HEAD_DIM)


def spread(lines, count):
    n = lines.shape[0]
    shape = (count * n, n * HEAD_DIM)
    line = lax.broadcasted_iota(jnp.int32, shape, 0) % n
    head = lax.broadcasted_iota(jnp.int32, shape, 1) // HEAD_DIM
    pick = (line == head).astype(F32).astype(BF16)
    return dot(jnp.concatenate(parts(lines, count), axis=0), pick, 0, 0)


def latest_of(rows):
    return rows[8:9, :]


def outward_of(rows, slots):
    row, latest = rows[slots, :], latest_of(rows)
    place = lax.broadcasted_iota(jnp.int32, row.shape, 1).astype(F32)
    kept = place >= latest[:, TOK - 1 : TOK]
    return jnp.exp(jnp.where(kept, row[:, TOK - 1 : TOK] - row, NEG))


def inward_of(rows):
    return jnp.exp(jnp.where(latest_of(rows) < 0, rows[0:8, :], NEG))


def through_of(rows):
    last = jnp.where(latest_of(rows)[:, TOK - 1 : TOK] < 0, rows[0:8, TOK - 1 : TOK], NEG)
    return jnp.broadcast_to(jnp.exp(last), (8, HEAD_DIM))


def turn(left, line):
    return (left.T.astype(F32) * line).astype(BF16)


def fetch(pairs, sems):
    copies = [pltpu.make_async_copy(src, dst, sems.at[n]) for n, (src, dst) in enumerate(pairs)]
    for copy in copies:
        copy.start()
    return copies


def k_first(
    core_ref, starts_in, decay, q, k, v, send, rows, q_mine, k_mine, v_mine, kbuf, vbuf, dbuf, starts, sems
):
    core = core_ref[0]
    there = half_cols(1 - core)
    mine = half_cols(core)
    copies = fetch(
        [
            (decay, dbuf), (starts_in, starts), (k.at[:, there], kbuf), (v.at[:, there], vbuf),
            (k.at[:, mine], k_mine), (v.at[:, mine], v_mine), (q.at[:, mine], q_mine),
        ],
        sems,
    )
    a = lax.broadcasted_iota(jnp.int32, (TOK, TOK), 0)
    b = lax.broadcasted_iota(jnp.int32, (TOK, TOK), 1)
    copies[0].wait()
    d = dbuf[...]
    d = jnp.where(core == 0, d, jnp.concatenate([d[HALF:], d[:HALF]], axis=0))
    sums = dot(jnp.concatenate(parts(d, 3), axis=0), (a <= b).astype(BF16), 1, 0)
    rows[0:8, :] = sums[0:8] + sums[8:16] + sums[16:24]
    copies[1].wait()
    place = lax.broadcasted_iota(jnp.int32, (8, TOK), 1)
    latest = jnp.full((8, TOK), -1, jnp.int32)
    for j in range(4):
        begin = starts[0, j]
        latest = jnp.maximum(latest, jnp.where(begin <= place, begin, -1))
    rows[8:16, :] = latest.astype(F32)
    outward = outward_of(rows, slice(HALF, 8))
    through = through_of(rows)
    send[512:520, :] = jnp.concatenate([through[HALF:8], through[0:HALF]], axis=0)
    copies[2].wait()
    copies[3].wait()
    for i in range(HALF):
        turned = turn(kbuf[:, here(i)], outward[i : i + 1, :])
        send[i * 128 : (i + 1) * 128, :] = dot(turned, vbuf[:, here(i)], 1, 0)
    for copy in copies[4:]:
        copy.wait()


def mixed(weight, query, key, value):
    return dot((weight * dot(query, key, 1, 1)).astype(BF16), value, 1, 0)


def biases(rows):
    latest = spread(latest_of(rows), 1)
    t = lax.broadcasted_iota(jnp.int32, (TOK, HEAD_DIM), 0)
    s = lax.broadcasted_iota(jnp.int32, (TOK, HEAD_DIM), 1)
    out = []
    for part in range(2):
        place = s + part * HEAD_DIM
        out.append(jnp.where(jnp.logical_and(place <= t, place.astype(F32) >= latest), 0.0, NEG))
    return out


def weight_of(rows, column, bias, slot):
    line = rows[slot : slot + 1, :]
    return jnp.concatenate(
        [jnp.exp(column - line[:, here(part)] + bias[part]) for part in range(2)], axis=1
    )


def k_local(rows, q, k, v, mine, within, summed, inward):
    inward[...] = spread(inward_of(rows), 2)
    columns = spread(rows[0:8, :], 3)
    summed[...] = columns
    bias = biases(rows)
    outward = outward_of(rows, slice(0, HALF))
    mine[512:520, :] = through_of(rows)
    for i in range(HALF):
        turned = turn(k[:, here(i)], outward[i : i + 1, :])
        mine[i * 128 : (i + 1) * 128, :] = dot(turned, v[:, here(i)], 1, 0)
    for i in range(HALF):
        weight = weight_of(rows, columns[:, here(i)], bias, i)
        within[:, here(i)] = mixed(weight, q[:, here(i)], k[:, here(i)], v[:, here(i)])


def k_pack(core_ref, mine, other, out):
    first = core_ref[0] == 0
    for i in range(HALF):
        at = slice(i * 128, (i + 1) * 128)
        g_mine, g_other = mine[512 + i : 513 + i, :], other[512 + i : 513 + i, :]
        s_mine, s_other = mine[at, :], other[at, :]
        state = jnp.where(first, s_mine * g_other + s_other, s_other * g_mine + s_mine)
        for j in range(8):
            base = 17 * (8 * i + j)
            out[base : base + 16, :] = state[16 * j : 16 * (j + 1), :]
            out[base + 16 : base + 17, :] = g_mine * g_other


def k_scan(pieces, out):
    state = jnp.zeros((16, HEAD_DIM), F32)
    for i in range(32):
        out[i] = state
        state = state * pieces[17 * i + 16 : 17 * i + 17, :] + pieces[17 * i : 17 * i + 16, :]


def k_scan_back(pieces, factors, out):
    state = jnp.zeros((16, HEAD_DIM), F32)
    for i in reversed(range(32)):
        out[i] = state
        state = state * factors[17 * i + 16 : 17 * i + 17, :] + pieces[i]


def k_enter(core_ref, entering, mine, other, e_mine, e_send):
    first = core_ref[0] == 0
    for i in range(HALF):
        at = slice(i * 128, (i + 1) * 128)
        g0 = jnp.where(first, mine[512 + i : 513 + i, :], other[512 + i : 513 + i, :])
        s0 = jnp.where(first, mine[at, :], other[at, :])
        e0 = entering[at, :]
        e1 = e0 * g0 + s0
        e_mine[at, :] = jnp.where(first, e0, e1)
        e_send[at, :] = jnp.where(first, e1, e0)


def k_attend(
    core_ref, rows, summed, q, k, v, within, inward, e_mine, gate, gain, up,
    att_mine, dnormed, within_other, part,
):
    core = core_ref[0]
    bias = biases(rows)
    squares = jnp.zeros((TOK, HEAD_DIM), F32)
    products = jnp.zeros((TOK, HEAD_DIM), F32)
    for slot in range(8):
        at = cols(core, slot)
        dn = up[:, at].astype(F32) * gain[:, at] * jax.nn.sigmoid(gate[:, at].astype(F32))
        dnormed[:, here(slot)] = dn
        if slot < HALF:
            carried = wide_dot(q[:, at], e_mine[slot * 128 : (slot + 1) * 128, :], 0)
            att = within[:, here(slot)] + carried * inward[:, here(slot)]
            att_mine[:, here(slot)] = att
            squares += att * att
            products += dn * att
        else:
            weight = weight_of(rows, summed[:, here(slot)], bias, slot)
            within_other[:, here(slot - HALF)] = mixed(weight, q[:, at], k[:, at], v[:, at])
    part[0] = squares
    part[1] = products


def k_sums(core_ref, q, within, inward, e_other, part, dnormed, att_other, sums):
    core = core_ref[0]
    squares, products = part[0], part[1]
    for i in range(HALF):
        slot = HALF + i
        carried = wide_dot(q[:, cols(core, slot)], e_other[i * 128 : (i + 1) * 128, :], 0)
        att = within[:, here(i)] + carried * inward[:, here(slot)]
        att_other[:, here(i)] = att
        squares += att * att
        products += dnormed[:, here(slot)] * att
    ones = jnp.ones((8, 2 * HEAD_DIM), BF16)
    line = lax.broadcasted_iota(jnp.int32, (8, TOK), 0)
    sums[...] = jnp.where(
        line < 4,
        dot(ones, jnp.concatenate(parts(squares, 2), axis=1), 1, 1),
        dot(ones, jnp.concatenate(parts(products, 2), axis=1), 1, 1),
    )


def k_mid(
    core_ref, rows, summed, q, k, gate, att_mine, att_other, dnormed,
    weights, turned, mixings, factor, scaled, outward,
):
    core = core_ref[0]
    latest = latest_of(rows)
    outward[...] = spread(outward_of(rows, slice(0, 8)), 2)
    biased = biases(rows)
    for slot in range(8):
        weights[slot] = weight_of(rows, summed[:, here(slot)], biased, slot)
    s = lax.broadcasted_iota(jnp.int32, (TOK, HEAD_DIM), 0)
    t = lax.broadcasted_iota(jnp.int32, (TOK, HEAD_DIM), 1)
    for part in range(2):
        at = here(part)
        kept = jnp.logical_and(s <= t + part * HEAD_DIM, s.astype(F32) >= latest[:, at])
        bias = jnp.where(kept, 0.0, NEG)
        for slot in range(8):
            turned[slot, :, at] = jnp.exp(rows[slot : slot + 1, at] - summed[:, here(slot)] + bias)
    lines = inward_of(rows)
    for slot in reversed(range(8)):
        at = cols(core, slot)
        i = slot % HALF
        query = q[:, at]
        scaled[slot] = turn(query, lines[slot : slot + 1, :])
        mixings[slot] = (turned[slot] * dot(k[:, at], query, 1, 1)).astype(BF16)
        att = (att_mine if slot < HALF else att_other)[:, here(i)]
        opening = jax.nn.sigmoid(gate[:, at].astype(F32))
        factor[:, here(slot)] = dnormed[:, here(slot)] * att * (1.0 - opening)


def grad_of(att, dnormed, inverse, projection):
    return ((dnormed - att * inverse * projection) * inverse).astype(BF16)


def k_grad(sums0, sums1, sums2, sums3, att, dnormed, scaled, grad, send, inverses, projections, *, features):
    total = sums0[...] + sums1[...] + sums2[...] + sums3[...]
    inverse = 1.0 / jnp.sqrt(total[0:1] / features + EPSILON)
    both = spread(jnp.concatenate([inverse, total[4:5] * inverse / features], axis=0), 3)
    inverse, projection = both[:, :HEAD_DIM], both[:, HEAD_DIM:]
    for i in range(HALF):
        slot = HALF + i
        value = grad_of(att[:, here(i)], dnormed[:, here(slot)], inverse, projection)
        grad[:, here(i)] = value
        send[i * 128 : (i + 1) * 128, :] = dot(scaled[slot], value, 1, 0)
    inverses[...] = inverse
    projections[...] = projection


def query_of(grad_mixing, key, upstream, states, inward, slot):
    i = slot % HALF
    carried = wide_dot(upstream, states[i * 128 : (i + 1) * 128, :], 1)
    return (dot(grad_mixing, key, 1, 0) + carried * inward[:, here(slot)]).astype(BF16)


def k_back(
    core_ref, inverses, projections, att_mine, dnormed, grad_other, k, v,
    weights, turned, factor, inward, scaled, e_mine,
    mine, grad_mine, gq, gate_out, mixed_back, held,
):
    core = core_ref[0]
    inverse, projection = inverses[...], projections[...]
    for slot in range(8):
        at = cols(core, slot)
        i = slot % HALF
        key, value = k[:, at], v[:, at]
        if slot < HALF:
            upstream = grad_of(att_mine[:, here(i)], dnormed[:, here(slot)], inverse, projection)
            grad_mine[:, here(i)] = upstream
            mine[i * 128 : (i + 1) * 128, :] = dot(scaled[slot], upstream, 1, 0)
        else:
            upstream = grad_other[:, here(i)]
        grad_mixing = (weights[slot] * dot(upstream, value, 1, 1)).astype(BF16)
        mixed_back[slot] = (turned[slot] * dot(value, upstream, 1, 1)).astype(BF16)
        if slot < HALF:
            gq[:, here(i)] = query_of(grad_mixing, key, upstream, e_mine, inward, slot)
        else:
            held[i] = grad_mixing
        gate_out[:, at] = (factor[:, here(slot)] * inverse).astype(BF16)


def k_pack_back(core_ref, mine, other, s_mine, s_other, out):
    first = core_ref[0] == 0
    for i in range(HALF):
        at = slice(i * 128, (i + 1) * 128)
        g0 = jnp.where(first, s_mine[512 + i : 513 + i, :], s_other[512 + i : 513 + i, :])
        b_mine, b_other = mine[at, :], other[at, :]
        state = jnp.where(first, b_mine + g0 * b_other, b_other + g0 * b_mine)
        for j in range(8):
            out[8 * i + j] = state[16 * j : 16 * (j + 1), :]


def k_leave(core_ref, leaving, mine, other, s_mine, s_other, l_mine, l_send):
    first = core_ref[0] == 0
    for i in range(HALF):
        at = slice(i * 128, (i + 1) * 128)
        g1 = jnp.where(first, s_other[512 + i : 513 + i, :], s_mine[512 + i : 513 + i, :])
        b1 = jnp.where(first, other[at, :], mine[at, :])
        l1 = leaving[at, :]
        l0 = l1 * g1 + b1
        l_mine[at, :] = jnp.where(first, l0, l1)
        l_send[at, :] = jnp.where(first, l1, l0)


def finish(state, scale, key, value, part_k, part_v):
    to_key = wide_dot(value, state, 1)
    to_value = wide_dot(key, state, 0)
    return (part_k + to_key * scale).astype(BF16), (part_v + to_value * scale).astype(BF16)


def upper_dot(mixed_to, slot, right):
    half = TOK // 2
    return jnp.concatenate(
        [
            dot(mixed_to[slot, :half, :], right, 1, 0),
            dot(mixed_to[slot, half:, half:], right[half:], 1, 0),
        ],
        axis=0,
    )


def k_end_mine(
    core_ref, outward, q, k, v, grad_mine, grad_other, mixed_back, mixings, l_mine, held, inward, e_other,
    part_k, part_v, k_mine, v_mine, q_other,
):
    core = core_ref[0]
    for slot in range(8):
        i = slot % HALF
        at = cols(core, slot)
        upstream = (grad_mine if slot < HALF else grad_other)[:, here(i)]
        to_key = upper_dot(mixed_back, slot, q[:, at])
        to_value = upper_dot(mixings, slot, upstream)
        if slot < HALF:
            state = l_mine[i * 128 : (i + 1) * 128, :]
            k_mine[:, here(i)], v_mine[:, here(i)] = finish(
                state, outward[:, here(slot)], k[:, at], v[:, at], to_key, to_value
            )
        else:
            part_k[:, here(i)] = to_key
            part_v[:, here(i)] = to_value
            q_other[:, here(i)] = query_of(held[i], k[:, at], upstream, e_other, inward, slot)


def k_end(
    core_ref, outward, k, v, part_k, part_v, l_other, k_mine, v_mine, q_mine, q_other, gate_in,
    out_k, out_v, out_q, out_gate, kbuf, vbuf, sems,
):
    core = core_ref[0]
    there = half_cols(core)
    copies = fetch(
        [(k_mine, out_k.at[:, there]), (v_mine, out_v.at[:, there]), (q_mine, out_q.at[:, there]), (q_other, out_q.at[:, half_cols(1 - core)]), (gate_in, out_gate)],
        sems,
    )
    for i in range(HALF):
        slot = HALF + i
        at = cols(core, slot)
        state = l_other[i * 128 : (i + 1) * 128, :]
        kbuf[:, here(i)], vbuf[:, here(i)] = finish(
            state, outward[:, here(slot)], k[:, at], v[:, at], part_k[:, here(i)], part_v[:, here(i)]
        )
        for n, (buf, out) in enumerate(((kbuf, out_k), (vbuf, out_v))):
            copies.append(pltpu.make_async_copy(buf.at[:, here(i)], out.at[:, at], sems.at[5 + 2 * i + n]))
            copies[-1].start()
    for copy in copies:
        copy.wait()


def local(q, k, v, decay, starts, gate, gain, up):
    places = lax.axis_size("seq")
    swap = [(i, i ^ 1) for i in range(places)]
    groups = [list(range(c, places, 2)) for c in range(2)]
    core = (lax.axis_index("seq") % 2).astype(jnp.int32).reshape(1)
    heads = lax.axis_size("head")
    features = q.shape[1] * heads
    gain = gain.reshape(1, -1)
    wide, half = (TOK, 1024), (TOK, 512)
    state, state_g = (512, HEAD_DIM), (520, HEAD_DIM)
    square = (8, TOK, TOK)
    buffer = pltpu.VMEM(half, BF16)

    def trade(a):
        return lax.all_to_all(a, "seq", 0, 0, axis_index_groups=groups)

    def around(a, step):
        return lax.ppermute(a, "head", [(i, (i + step) % heads) for i in range(heads)])

    send, rows, *own = call(
        k_first,
        [(state_g, F32), ((16, TOK), F32)] + [(half, BF16)] * 3,
        1, core, starts, decay, q, k, v,
        hbm=(1, 2, 3, 4, 5),
        scratch=[
            buffer, buffer, pltpu.VMEM((8, TOK), F32), pltpu.SMEM((1, 4), jnp.int32), pltpu.SemaphoreType.DMA((7,)),
        ],
    )
    s_other = lax.ppermute(send, "seq", swap)
    s_mine, within, summed, inward = call(
        k_local,
        [(state_g, F32), (half, F32), (wide, F32), (wide, F32)],
        0, rows, *own,
    )
    (pieces,) = call(k_pack, [((544, HEAD_DIM), F32)], 1, core, s_mine, s_other)
    pieces = trade(pieces.reshape(32, 1, 17 * HEAD_DIM)).reshape(544, HEAD_DIM)
    (entering,) = call(k_scan, [((32, 16, HEAD_DIM), F32)], 0, pieces)
    entering = trade(entering).reshape(state)
    e_mine, e_send = call(k_enter, [(state, F32)] * 2, 1, core, entering, s_mine, s_other)
    e_other = lax.ppermute(e_send, "seq", swap)
    att_mine, dnormed, within_other, part = call(
        k_attend,
        [(half, F32), (wide, F32), (half, F32), ((2, TOK, HEAD_DIM), F32)],
        1, core, rows, summed, q, k, v, within, inward, e_mine, gate, gain, up,
    )
    att_other, sums = call(
        k_sums,
        [(half, F32), ((8, TOK), F32)],
        1, core, q, within_other, inward, e_other, part, dnormed,
    )
    others = [around(sums, step) for step in (2, 1, 3)]
    weights, turned, mixings, factor, scaled, outward = call(
        k_mid,
        [(square, F32), (square, F32), (square, BF16), (wide, F32), ((8, HEAD_DIM, TOK), BF16), (wide, F32)],
        1, core, rows, summed, q, k, gate, att_mine, att_other, dnormed,
        cost_estimate=pl.CostEstimate(flops=4_000_000_000, bytes_accessed=8_000_000, transcendentals=1_000_000),
    )
    grad_other, b_send, inverses, projections = call(
        functools.partial(k_grad, features=float(features)),
        [(half, BF16), (state, F32), ((TOK, HEAD_DIM), F32), ((TOK, HEAD_DIM), F32)],
        0, sums, *others, att_other, dnormed, scaled,
    )
    b_other = lax.ppermute(b_send, "seq", swap)
    b_mine, grad_mine, gq, grad_gate, mixed_back, held = call(
        k_back,
        [(state, F32), (half, BF16), (half, BF16), (wide, BF16), (square, BF16), ((HALF, TOK, TOK), BF16)],
        1, core, inverses, projections, att_mine, dnormed, grad_other, k, v,
        weights, turned, factor, inward, scaled, e_mine,
    )
    (back,) = call(k_pack_back, [((32, 16, HEAD_DIM), F32)], 1, core, b_mine, b_other, s_mine, s_other)
    back = trade(back)
    (leaving,) = call(k_scan_back, [((32, 16, HEAD_DIM), F32)], 0, back, pieces)
    leaving = trade(leaving).reshape(state)
    l_mine, l_send = call(k_leave, [(state, F32)] * 2, 1, core, leaving, b_mine, b_other, s_mine, s_other)
    l_other = lax.ppermute(l_send, "seq", swap)
    part_k, part_v, k_mine, v_mine, q_other = call(
        k_end_mine,
        [(half, F32), (half, F32), (half, BF16), (half, BF16), (half, BF16)],
        1, core, outward, q, k, v, grad_mine, grad_other, mixed_back, mixings, l_mine,
        held, inward, e_other,
    )
    grad_key, grad_value, grad_query, grad_gate = call(
        k_end,
        [(wide, BF16)] * 4,
        1, core, outward, k, v, part_k, part_v, l_other, k_mine, v_mine, gq, q_other, grad_gate,
        hbm_out=(0, 1, 2, 3),
        scratch=[buffer, buffer, pltpu.SemaphoreType.DMA((13,))],
    )
    return grad_query, grad_key, grad_value, grad_gate


def solution(mesh):
    token = P("seq", "head")
    return jax.shard_map(
        local,
        mesh=mesh,
        in_specs=(token, token, token, P("head", "seq"), P("seq", None), token, P("head"), token),
        out_specs=(token,) * 4,
        check_vma=False,
    )
```

```python
import functools

import jax
import jax.numpy as jnp
from jax import lax
from jax.experimental import pallas as pl
from jax.experimental.pallas import tpu as pltpu
from jax.sharding import PartitionSpec as P

HEAD_DIM = 128
TOK = 256
HALF = 4
EPSILON = 1e-06
F32 = jnp.float32
BF16 = jnp.bfloat16
NEG = -1e30


def dot(a, b, ca, cb):
    return lax.dot_general(a, b, (((ca,), (cb,)), ((), ())), preferred_element_type=F32)


def parts(a, count):
    out = []
    for _ in range(count):
        out.append(a.astype(BF16))
        a = a - out[-1].astype(F32)
    return out


def wide_dot(a, state, axis):
    return dot(jnp.concatenate([a, a], axis=1), jnp.concatenate(parts(state, 2), axis=axis), 1, axis)


def call(kernel, outs, n_smem, *args, hbm=(), hbm_out=(), scratch=(), **kw):
    smem = pl.BlockSpec(memory_space=pltpu.SMEM)
    vmem = pl.BlockSpec(memory_space=pltpu.VMEM)
    far = pl.BlockSpec(memory_space=pltpu.HBM)
    args = [pltpu.with_memory_space_constraint(a, pltpu.HBM) if n in hbm else a for n, a in enumerate(args)]
    return pl.pallas_call(
        kernel,
        out_shape=[jax.ShapeDtypeStruct(s, d) for s, d in outs],
        in_specs=[smem] * n_smem + [far if n in hbm else vmem for n in range(n_smem, len(args))],
        out_specs=[far if n in hbm_out else vmem for n in range(len(outs))],
        scratch_shapes=list(scratch),
        compiler_params=pltpu.CompilerParams(vmem_limit_bytes=24 * 1024 * 1024),
        **kw,
    )(*args)


def cols(core, slot):
    return pl.ds(pl.multiple_of(((slot + HALF * core) % 8) * HEAD_DIM, HEAD_DIM), HEAD_DIM)


def half_cols(half):
    width = HALF * HEAD_DIM
    return pl.ds(pl.multiple_of(half * width, width), width)


def here(slot):
    return slice(slot * HEAD_DIM, (slot + 1) * HEAD_DIM)


def spread(lines, count):
    n = lines.shape[0]
    shape = (count * n, n * HEAD_DIM)
    line = lax.broadcasted_iota(jnp.int32, shape, 0) % n
    head = lax.broadcasted_iota(jnp.int32, shape, 1) // HEAD_DIM
    pick = (line == head).astype(F32).astype(BF16)
    return dot(jnp.concatenate(parts(lines, count), axis=0), pick, 0, 0)


def latest_of(rows):
    return rows[8:9, :]


def outward_of(rows, slots):
    row, latest = rows[slots, :], latest_of(rows)
    place = lax.broadcasted_iota(jnp.int32, row.shape, 1).astype(F32)
    kept = place >= latest[:, TOK - 1 : TOK]
    return jnp.exp(jnp.where(kept, row[:, TOK - 1 : TOK] - row, NEG))


def inward_of(rows):
    return jnp.exp(jnp.where(latest_of(rows) < 0, rows[0:8, :], NEG))


def through_of(rows):
    last = jnp.where(latest_of(rows)[:, TOK - 1 : TOK] < 0, rows[0:8, TOK - 1 : TOK], NEG)
    return jnp.broadcast_to(jnp.exp(last), (8, HEAD_DIM))


def turn(left, line):
    return (left.T.astype(F32) * line).astype(BF16)


def fetch(pairs, sems):
    copies = [pltpu.make_async_copy(src, dst, sems.at[n]) for n, (src, dst) in enumerate(pairs)]
    for copy in copies:
        copy.start()
    return copies


def k_first(
    core_ref, starts_in, decay, q, k, v, send, rows, q_mine, k_mine, v_mine, kbuf, vbuf, dbuf, starts, sems
):
    core = core_ref[0]
    there = half_cols(1 - core)
    mine = half_cols(core)
    copies = fetch(
        [
            (decay, dbuf), (starts_in, starts), (k.at[:, there], kbuf), (v.at[:, there], vbuf),
            (k.at[:, mine], k_mine), (v.at[:, mine], v_mine), (q.at[:, mine], q_mine),
        ],
        sems,
    )
    a = lax.broadcasted_iota(jnp.int32, (TOK, TOK), 0)
    b = lax.broadcasted_iota(jnp.int32, (TOK, TOK), 1)
    copies[0].wait()
    d = dbuf[...]
    d = jnp.where(core == 0, d, jnp.concatenate([d[HALF:], d[:HALF]], axis=0))
    sums = dot(jnp.concatenate(parts(d, 3), axis=0), (a <= b).astype(BF16), 1, 0)
    rows[0:8, :] = sums[0:8] + sums[8:16] + sums[16:24]
    copies[1].wait()
    place = lax.broadcasted_iota(jnp.int32, (8, TOK), 1)
    latest = jnp.full((8, TOK), -1, jnp.int32)
    for j in range(4):
        begin = starts[0, j]
        latest = jnp.maximum(latest, jnp.where(begin <= place, begin, -1))
    rows[8:16, :] = latest.astype(F32)
    outward = outward_of(rows, slice(HALF, 8))
    through = through_of(rows)
    send[512:520, :] = jnp.concatenate([through[HALF:8], through[0:HALF]], axis=0)
    copies[2].wait()
    copies[3].wait()
    for i in range(HALF):
        turned = turn(kbuf[:, here(i)], outward[i : i + 1, :])
        send[i * 128 : (i + 1) * 128, :] = dot(turned, vbuf[:, here(i)], 1, 0)
    for copy in copies[4:]:
        copy.wait()


def mixed(weight, query, key, value):
    return dot((weight * dot(query, key, 1, 1)).astype(BF16), value, 1, 0)


def biases(rows):
    latest = spread(latest_of(rows), 1)
    t = lax.broadcasted_iota(jnp.int32, (TOK, HEAD_DIM), 0)
    s = lax.broadcasted_iota(jnp.int32, (TOK, HEAD_DIM), 1)
    out = []
    for part in range(2):
        place = s + part * HEAD_DIM
        out.append(jnp.where(jnp.logical_and(place <= t, place.astype(F32) >= latest), 0.0, NEG))
    return out


def weight_of(rows, column, bias, slot):
    line = rows[slot : slot + 1, :]
    return jnp.concatenate(
        [jnp.exp(column - line[:, here(part)] + bias[part]) for part in range(2)], axis=1
    )


def k_local(rows, q, k, v, mine, within, summed, inward):
    inward[...] = spread(inward_of(rows), 2)
    columns = spread(rows[0:8, :], 3)
    summed[...] = columns
    bias = biases(rows)
    outward = outward_of(rows, slice(0, HALF))
    mine[512:520, :] = through_of(rows)
    for i in range(HALF):
        turned = turn(k[:, here(i)], outward[i : i + 1, :])
        mine[i * 128 : (i + 1) * 128, :] = dot(turned, v[:, here(i)], 1, 0)
    for i in range(HALF):
        weight = weight_of(rows, columns[:, here(i)], bias, i)
        within[:, here(i)] = mixed(weight, q[:, here(i)], k[:, here(i)], v[:, here(i)])


def k_pack(core_ref, mine, other, out):
    first = core_ref[0] == 0
    for i in range(HALF):
        at = slice(i * 128, (i + 1) * 128)
        g_mine, g_other = mine[512 + i : 513 + i, :], other[512 + i : 513 + i, :]
        s_mine, s_other = mine[at, :], other[at, :]
        state = jnp.where(first, s_mine * g_other + s_other, s_other * g_mine + s_mine)
        for j in range(8):
            base = 17 * (8 * i + j)
            out[base : base + 16, :] = state[16 * j : 16 * (j + 1), :]
            out[base + 16 : base + 17, :] = g_mine * g_other


def k_scan(pieces, out):
    state = jnp.zeros((16, HEAD_DIM), F32)
    for i in range(32):
        out[i] = state
        state = state * pieces[17 * i + 16 : 17 * i + 17, :] + pieces[17 * i : 17 * i + 16, :]


def k_scan_back(pieces, factors, out):
    state = jnp.zeros((16, HEAD_DIM), F32)
    for i in reversed(range(32)):
        out[i] = state
        state = state * factors[17 * i + 16 : 17 * i + 17, :] + pieces[i]


def k_enter(core_ref, entering, mine, other, e_mine, e_send):
    first = core_ref[0] == 0
    for i in range(HALF):
        at = slice(i * 128, (i + 1) * 128)
        g0 = jnp.where(first, mine[512 + i : 513 + i, :], other[512 + i : 513 + i, :])
        s0 = jnp.where(first, mine[at, :], other[at, :])
        e0 = entering[at, :]
        e1 = e0 * g0 + s0
        e_mine[at, :] = jnp.where(first, e0, e1)
        e_send[at, :] = jnp.where(first, e1, e0)


def k_attend(
    core_ref, rows, summed, q, k, v, within, inward, e_mine, gate, gain, up,
    att_mine, dnormed, within_other, part,
):
    core = core_ref[0]
    bias = biases(rows)
    squares = jnp.zeros((TOK, HEAD_DIM), F32)
    products = jnp.zeros((TOK, HEAD_DIM), F32)
    for slot in range(8):
        at = cols(core, slot)
        dn = up[:, at].astype(F32) * gain[:, at] * jax.nn.sigmoid(gate[:, at].astype(F32))
        dnormed[:, here(slot)] = dn
        if slot < HALF:
            carried = wide_dot(q[:, at], e_mine[slot * 128 : (slot + 1) * 128, :], 0)
            att = within[:, here(slot)] + carried * inward[:, here(slot)]
            att_mine[:, here(slot)] = att
            squares += att * att
            products += dn * att
        else:
            weight = weight_of(rows, summed[:, here(slot)], bias, slot)
            within_other[:, here(slot - HALF)] = mixed(weight, q[:, at], k[:, at], v[:, at])
    part[0] = squares
    part[1] = products


def k_sums(core_ref, q, within, inward, e_other, part, dnormed, att_other, sums):
    core = core_ref[0]
    squares, products = part[0], part[1]
    for i in range(HALF):
        slot = HALF + i
        carried = wide_dot(q[:, cols(core, slot)], e_other[i * 128 : (i + 1) * 128, :], 0)
        att = within[:, here(i)] + carried * inward[:, here(slot)]
        att_other[:, here(i)] = att
        squares += att * att
        products += dnormed[:, here(slot)] * att
    ones = jnp.ones((8, 2 * HEAD_DIM), BF16)
    line = lax.broadcasted_iota(jnp.int32, (8, TOK), 0)
    sums[...] = jnp.where(
        line < 4,
        dot(ones, jnp.concatenate(parts(squares, 2), axis=1), 1, 1),
        dot(ones, jnp.concatenate(parts(products, 2), axis=1), 1, 1),
    )


def k_mid(
    core_ref, rows, summed, q, k, gate, att_mine, att_other, dnormed,
    weights, turned, mixings, factor, scaled, outward,
):
    core = core_ref[0]
    latest = latest_of(rows)
    outward[...] = spread(outward_of(rows, slice(0, 8)), 2)
    biased = biases(rows)
    for slot in range(8):
        weights[slot] = weight_of(rows, summed[:, here(slot)], biased, slot)
    s = lax.broadcasted_iota(jnp.int32, (TOK, HEAD_DIM), 0)
    t = lax.broadcasted_iota(jnp.int32, (TOK, HEAD_DIM), 1)
    for part in range(2):
        at = here(part)
        kept = jnp.logical_and(s <= t + part * HEAD_DIM, s.astype(F32) >= latest[:, at])
        bias = jnp.where(kept, 0.0, NEG)
        for slot in range(8):
            turned[slot, :, at] = jnp.exp(rows[slot : slot + 1, at] - summed[:, here(slot)] + bias)
    lines = inward_of(rows)
    for slot in reversed(range(8)):
        at = cols(core, slot)
        i = slot % HALF
        query = q[:, at]
        scaled[slot] = turn(query, lines[slot : slot + 1, :])
        mixings[slot] = (turned[slot] * dot(k[:, at], query, 1, 1)).astype(BF16)
        att = (att_mine if slot < HALF else att_other)[:, here(i)]
        opening = jax.nn.sigmoid(gate[:, at].astype(F32))
        factor[:, here(slot)] = dnormed[:, here(slot)] * att * (1.0 - opening)


def grad_of(att, dnormed, inverse, projection):
    return ((dnormed - att * inverse * projection) * inverse).astype(BF16)


def k_grad(sums0, sums1, sums2, sums3, att, dnormed, scaled, grad, send, inverses, projections, *, features):
    total = sums0[...] + sums1[...] + sums2[...] + sums3[...]
    inverse = 1.0 / jnp.sqrt(total[0:1] / features + EPSILON)
    both = spread(jnp.concatenate([inverse, total[4:5] * inverse / features], axis=0), 3)
    inverse, projection = both[:, :HEAD_DIM], both[:, HEAD_DIM:]
    for i in range(HALF):
        slot = HALF + i
        value = grad_of(att[:, here(i)], dnormed[:, here(slot)], inverse, projection)
        grad[:, here(i)] = value
        send[i * 128 : (i + 1) * 128, :] = dot(scaled[slot], value, 1, 0)
    inverses[...] = inverse
    projections[...] = projection


def query_of(grad_mixing, key, upstream, states, inward, slot):
    i = slot % HALF
    carried = wide_dot(upstream, states[i * 128 : (i + 1) * 128, :], 1)
    return (dot(grad_mixing, key, 1, 0) + carried * inward[:, here(slot)]).astype(BF16)


def k_back(
    core_ref, inverses, projections, att_mine, dnormed, grad_other, k, v,
    weights, turned, factor, inward, scaled, e_mine,
    mine, grad_mine, gq, gate_out, mixed_back, held,
):
    core = core_ref[0]
    inverse, projection = inverses[...], projections[...]
    for slot in range(8):
        at = cols(core, slot)
        i = slot % HALF
        key, value = k[:, at], v[:, at]
        if slot < HALF:
            upstream = grad_of(att_mine[:, here(i)], dnormed[:, here(slot)], inverse, projection)
            grad_mine[:, here(i)] = upstream
            mine[i * 128 : (i + 1) * 128, :] = dot(scaled[slot], upstream, 1, 0)
        else:
            upstream = grad_other[:, here(i)]
        grad_mixing = (weights[slot] * dot(upstream, value, 1, 1)).astype(BF16)
        mixed_back[slot] = (turned[slot] * dot(value, upstream, 1, 1)).astype(BF16)
        if slot < HALF:
            gq[:, here(i)] = query_of(grad_mixing, key, upstream, e_mine, inward, slot)
        else:
            held[i] = grad_mixing
        gate_out[:, at] = (factor[:, here(slot)] * inverse).astype(BF16)


def k_pack_back(core_ref, mine, other, s_mine, s_other, out):
    first = core_ref[0] == 0
    for i in range(HALF):
        at = slice(i * 128, (i + 1) * 128)
        g0 = jnp.where(first, s_mine[512 + i : 513 + i, :], s_other[512 + i : 513 + i, :])
        b_mine, b_other = mine[at, :], other[at, :]
        state = jnp.where(first, b_mine + g0 * b_other, b_other + g0 * b_mine)
        for j in range(8):
            out[8 * i + j] = state[16 * j : 16 * (j + 1), :]


def k_leave(core_ref, leaving, mine, other, s_mine, s_other, l_mine, l_send):
    first = core_ref[0] == 0
    for i in range(HALF):
        at = slice(i * 128, (i + 1) * 128)
        g1 = jnp.where(first, s_other[512 + i : 513 + i, :], s_mine[512 + i : 513 + i, :])
        b1 = jnp.where(first, other[at, :], mine[at, :])
        l1 = leaving[at, :]
        l0 = l1 * g1 + b1
        l_mine[at, :] = jnp.where(first, l0, l1)
        l_send[at, :] = jnp.where(first, l1, l0)


def finish(state, scale, key, value, part_k, part_v):
    to_key = wide_dot(value, state, 1)
    to_value = wide_dot(key, state, 0)
    return (part_k + to_key * scale).astype(BF16), (part_v + to_value * scale).astype(BF16)


def upper_dot(mixed_to, slot, right):
    half = TOK // 2
    return jnp.concatenate(
        [
            dot(mixed_to[slot, :half, :], right, 1, 0),
            dot(mixed_to[slot, half:, half:], right[half:], 1, 0),
        ],
        axis=0,
    )


def k_end_mine(
    core_ref, outward, q, k, v, grad_mine, grad_other, mixed_back, mixings, l_mine, held, inward, e_other,
    part_k, part_v, k_mine, v_mine, q_other,
):
    core = core_ref[0]
    for slot in range(8):
        i = slot % HALF
        at = cols(core, slot)
        upstream = (grad_mine if slot < HALF else grad_other)[:, here(i)]
        to_key = upper_dot(mixed_back, slot, q[:, at])
        to_value = upper_dot(mixings, slot, upstream)
        if slot < HALF:
            state = l_mine[i * 128 : (i + 1) * 128, :]
            k_mine[:, here(i)], v_mine[:, here(i)] = finish(
                state, outward[:, here(slot)], k[:, at], v[:, at], to_key, to_value
            )
        else:
            part_k[:, here(i)] = to_key
            part_v[:, here(i)] = to_value
            q_other[:, here(i)] = query_of(held[i], k[:, at], upstream, e_other, inward, slot)


def k_end(
    core_ref, outward, k, v, part_k, part_v, l_other, k_mine, v_mine, q_mine, q_other, gate_in,
    out_k, out_v, out_q, out_gate, kbuf, vbuf, sems,
):
    core = core_ref[0]
    there = half_cols(core)
    copies = fetch(
        [(k_mine, out_k.at[:, there]), (v_mine, out_v.at[:, there]), (q_mine, out_q.at[:, there]), (q_other, out_q.at[:, half_cols(1 - core)]), (gate_in, out_gate)],
        sems,
    )
    for i in range(HALF):
        slot = HALF + i
        at = cols(core, slot)
        state = l_other[i * 128 : (i + 1) * 128, :]
        kbuf[:, here(i)], vbuf[:, here(i)] = finish(
            state, outward[:, here(slot)], k[:, at], v[:, at], part_k[:, here(i)], part_v[:, here(i)]
        )
        if i % 2 == 0:
            continue
        pair = slice((i - 1) * HEAD_DIM, (i + 1) * HEAD_DIM)
        begin = pl.multiple_of((1 - core) * 512 + (i - 1) * HEAD_DIM, 2 * HEAD_DIM)
        for n, (buf, out) in enumerate(((kbuf, out_k), (vbuf, out_v))):
            target = out.at[:, pl.ds(begin, 2 * HEAD_DIM)]
            copies.append(pltpu.make_async_copy(buf.at[:, pair], target, sems.at[5 + 2 * i + n]))
            copies[-1].start()
    for copy in copies:
        copy.wait()


def local(q, k, v, decay, starts, gate, gain, up):
    places = lax.axis_size("seq")
    swap = [(i, i ^ 1) for i in range(places)]
    groups = [list(range(c, places, 2)) for c in range(2)]
    core = (lax.axis_index("seq") % 2).astype(jnp.int32).reshape(1)
    heads = lax.axis_size("head")
    features = q.shape[1] * heads
    gain = gain.reshape(1, -1)
    wide, half = (TOK, 1024), (TOK, 512)
    state, state_g = (512, HEAD_DIM), (520, HEAD_DIM)
    square = (8, TOK, TOK)
    buffer = pltpu.VMEM(half, BF16)

    def trade(a):
        return lax.all_to_all(a, "seq", 0, 0, axis_index_groups=groups)

    def around(a, step):
        return lax.ppermute(a, "head", [(i, (i + step) % heads) for i in range(heads)])

    send, rows, *own = call(
        k_first,
        [(state_g, F32), ((16, TOK), F32)] + [(half, BF16)] * 3,
        1, core, starts, decay, q, k, v,
        hbm=(1, 2, 3, 4, 5),
        scratch=[
            buffer, buffer, pltpu.VMEM((8, TOK), F32), pltpu.SMEM((1, 4), jnp.int32), pltpu.SemaphoreType.DMA((7,)),
        ],
    )
    s_other = lax.ppermute(send, "seq", swap)
    s_mine, within, summed, inward = call(
        k_local,
        [(state_g, F32), (half, F32), (wide, F32), (wide, F32)],
        0, rows, *own,
    )
    (pieces,) = call(k_pack, [((544, HEAD_DIM), F32)], 1, core, s_mine, s_other)
    pieces = trade(pieces.reshape(32, 1, 17 * HEAD_DIM)).reshape(544, HEAD_DIM)
    (entering,) = call(k_scan, [((32, 16, HEAD_DIM), F32)], 0, pieces)
    entering = trade(entering).reshape(state)
    e_mine, e_send = call(k_enter, [(state, F32)] * 2, 1, core, entering, s_mine, s_other)
    e_other = lax.ppermute(e_send, "seq", swap)
    att_mine, dnormed, within_other, part = call(
        k_attend,
        [(half, F32), (wide, F32), (half, F32), ((2, TOK, HEAD_DIM), F32)],
        1, core, rows, summed, q, k, v, within, inward, e_mine, gate, gain, up,
    )
    att_other, sums = call(
        k_sums,
        [(half, F32), ((8, TOK), F32)],
        1, core, q, within_other, inward, e_other, part, dnormed,
    )
    others = [around(sums, step) for step in (2, 1, 3)]
    weights, turned, mixings, factor, scaled, outward = call(
        k_mid,
        [(square, F32), (square, F32), (square, BF16), (wide, F32), ((8, HEAD_DIM, TOK), BF16), (wide, F32)],
        1, core, rows, summed, q, k, gate, att_mine, att_other, dnormed,
        cost_estimate=pl.CostEstimate(flops=4_000_000_000, bytes_accessed=8_000_000, transcendentals=1_000_000),
    )
    grad_other, b_send, inverses, projections = call(
        functools.partial(k_grad, features=float(features)),
        [(half, BF16), (state, F32), ((TOK, HEAD_DIM), F32), ((TOK, HEAD_DIM), F32)],
        0, sums, *others, att_other, dnormed, scaled,
    )
    b_other = lax.ppermute(b_send, "seq", swap)
    b_mine, grad_mine, gq, grad_gate, mixed_back, held = call(
        k_back,
        [(state, F32), (half, BF16), (half, BF16), (wide, BF16), (square, BF16), ((HALF, TOK, TOK), BF16)],
        1, core, inverses, projections, att_mine, dnormed, grad_other, k, v,
        weights, turned, factor, inward, scaled, e_mine,
    )
    (back,) = call(k_pack_back, [((32, 16, HEAD_DIM), F32)], 1, core, b_mine, b_other, s_mine, s_other)
    back = trade(back)
    (leaving,) = call(k_scan_back, [((32, 16, HEAD_DIM), F32)], 0, back, pieces)
    leaving = trade(leaving).reshape(state)
    l_mine, l_send = call(k_leave, [(state, F32)] * 2, 1, core, leaving, b_mine, b_other, s_mine, s_other)
    l_other = lax.ppermute(l_send, "seq", swap)
    part_k, part_v, k_mine, v_mine, q_other = call(
        k_end_mine,
        [(half, F32), (half, F32), (half, BF16), (half, BF16), (half, BF16)],
        1, core, outward, q, k, v, grad_mine, grad_other, mixed_back, mixings, l_mine,
        held, inward, e_other,
    )
    grad_key, grad_value, grad_query, grad_gate = call(
        k_end,
        [(wide, BF16)] * 4,
        1, core, outward, k, v, part_k, part_v, l_other, k_mine, v_mine, gq, q_other, grad_gate,
        hbm_out=(0, 1, 2, 3),
        scratch=[buffer, buffer, pltpu.SemaphoreType.DMA((13,))],
    )
    return grad_query, grad_key, grad_value, grad_gate


def solution(mesh):
    token = P("seq", "head")
    return jax.shard_map(
        local,
        mesh=mesh,
        in_specs=(token, token, token, P("head", "seq"), P("seq", None), token, P("head"), token),
        out_specs=(token,) * 4,
        check_vma=False,
    )
```
